32 devices in a mesh: sub: 8 (over z, y), crs: 4 (over x, core).
Axes of the slice: x: 2, y: 2, z: 4, core: 2. Of those that a mesh axis runs over, the one named last changes fastest.
Arguments:
- dual_ops: bfloat16 [96, 1536, 1536], P('sub', 'crs')
- rigid_traces: float32 [96, 6, 1536], P('sub'), may hold values from -0.625 to 0.625
- coarse_factor: float32 [576, 576], P('sub', 'crs')
- partner: int32 [96, 12], P('sub'), may hold values from -1 to 287, as said below
- send_list: int32 [16, 72], P('sub'), may hold values from -1 to 143, as said below
- mode_count: int32 [96], P('sub'), may hold values from 0 to 6
- dual_rhs: float32 [96, 1536], P('sub'), may hold values from -6 to 6
- rigid_load: float32 [576], P('sub'), may hold values from -2400 to 2400
Outputs:
- multipliers: float32 [96, 1536], P('sub')
- projected_residual: float32 [96, 1536], P('sub')
The draws below stay inside these ranges and needn't reach their ends.
Inputs may be any that keep to these rules, and one draw needn't show every extreme that they name: For each block of a subdomain (subdomains in order, 12 blocks each): -1 for a padding block, else the position of its partner block in the list made of this index of sub's 12 * 12 blocks in order, then the 72 blocks received from the index before along sub, then the 72 from the index after. Partnership is mutual, never a block with itself, never across more than one index of sub. `send_list`: rows 2i and 2i+1 belong to index i of sub: its local blocks sent to the index before and to the index after, -1 in unused slots; the k-th block received from a neighbour is the k-th entry of that neighbour's row toward this index. The first index sends nothing before and the last nothing after; each boundary between neighbouring indices carries 72 // 2 to 72 blocks, one boundary exactly 72.
All inputs are finite; a program needn't handle non-finite values.
Results may differ from the reference program's by a relative error of at most 0.012.
The reference program's roundings to bfloat16 on the way count: a program that leaves them out, or rounds other values in their place, can miss the bound.
Values sent between devices are 32-bit elements; how exact they have to be, the bound alone decides.
No kernel may reach another device: no remote copies, remote signals or barrier semaphores. Data moves between devices by JAX's collectives and lax.ppermute only.
A program may use at most 64 MiB of HBM per device.

```python
import math
import jax
import jax.numpy as jnp
from jax import lax

SUB_DEV = 12
BLOCKS = 12
BLOCK = 128
MODES = 6
ITERATIONS = 2
ORDER = 1536
SLOTS = 72
SUBDOMAINS = 96
COARSE = 576
N_SUB = 8


def pairing(key):
    local_blocks = SUB_DEV * BLOCKS
    base_key = jax.random.fold_in(key, 7)
    count_key, pick_key, perm_key, local_key = jax.random.split(base_key, 4)
    crossing = jax.random.randint(count_key, (N_SUB - 1,), SLOTS // 2, SLOTS + 1)
    crossing = crossing.at[jax.random.randint(pick_key, (), 0, N_SUB - 1)].set(SLOTS)
    zero_one = jnp.zeros((1,), jnp.int32)
    left_count = jnp.concatenate([zero_one, crossing])
    right_count = jnp.concatenate([crossing, zero_one])
    perms = jax.vmap(lambda sub_key: jax.random.permutation(sub_key, local_blocks))(jax.random.split(perm_key, N_SUB))
    remain = local_blocks - left_count - right_count
    pair_count = jax.random.randint(local_key, (N_SUB,), remain // 4, remain // 2 + 1)
    position = jnp.arange(local_blocks, dtype=jnp.int32)[None, :]
    left_col = left_count[:, None]
    right_col = right_count[:, None]
    offset = position - left_col - right_col
    mate_pos = jnp.clip(left_col + right_col + jnp.bitwise_xor(jnp.maximum(offset, 0), 1), 0, local_blocks - 1)
    mate = jnp.take_along_axis(perms, mate_pos, axis=1)
    codes = jnp.where(position < left_col, local_blocks + position, jnp.where(position < left_col + right_col, local_blocks + SLOTS + position - left_col, jnp.where(offset < 2 * pair_count[:, None], mate, -1)))
    rows_idx = jnp.arange(N_SUB, dtype=jnp.int32)[:, None]
    partner_grid = jnp.zeros((N_SUB, local_blocks), jnp.int32).at[rows_idx, perms].set(codes.astype(jnp.int32))
    slot_idx = jnp.arange(SLOTS, dtype=jnp.int32)[None, :]
    to_before = jnp.where(slot_idx < left_col, perms[:, :SLOTS], -1)
    after_pos = jnp.clip(left_col + slot_idx, 0, local_blocks - 1)
    to_after = jnp.where(slot_idx < right_col, jnp.take_along_axis(perms, after_pos, axis=1), -1)
    sends = jnp.stack([to_before, to_after], axis=1).reshape(2 * N_SUB, SLOTS).astype(jnp.int32)
    return (partner_grid.reshape(SUB_DEV * N_SUB, BLOCKS), sends)


def draw_partner(key, part):
    return pairing(key)[0]


def draw_send_list(key, part):
    return pairing(key)[1]


def draw_dual_ops(key, part):
    order_len = BLOCKS * BLOCK

    def single(index):
        sub_key = jax.random.fold_in(jax.random.fold_in(key, 11), index)
        noise_key, diag_key = jax.random.split(sub_key)
        noise = jax.random.normal(noise_key, (order_len, order_len), jnp.float32)
        diagonal = jnp.exp(jax.random.uniform(diag_key, (order_len,), jnp.float32, math.log(1.5), math.log(4.0)))
        symmetric = (noise + noise.T) * (0.6 / math.sqrt(2.0 * order_len))
        return (symmetric + jnp.diag(diagonal)).astype(jnp.bfloat16)
    return lax.map(single, jnp.arange(SUB_DEV * N_SUB))


def draw_coarse_factor(key, part):
    coarse_len = MODES * SUB_DEV * N_SUB
    noise_key = jax.random.fold_in(key, 13)
    noise = jax.random.normal(noise_key, (coarse_len, coarse_len), jnp.float32)
    factor = 0.6 * jnp.eye(coarse_len, dtype=jnp.float32) + noise * (0.25 / math.sqrt(coarse_len))
    return 0.16 * factor


def touch_ends(values, key, low, high):
    longest = values.shape.index(max(values.shape))
    spots = []
    for shift in (0, 1):
        where = [jax.random.randint(jax.random.fold_in(key, axis), (), 0, length) for axis, length in enumerate(values.shape)]
        where[longest] = (where[longest] + shift) % values.shape[longest]
        spots.append(tuple(where))
    return values.at[spots[0]].set(low).at[spots[1]].set(high)


def block_levels(own_key, shape, shards, smallest, high):
    gain = 1.0
    for dim, blocks in shards:
        draws = jax.random.uniform(jax.random.fold_in(jax.random.fold_in(own_key, 6), dim), (blocks,), jnp.float32, smallest / len(shards), high / len(shards))
        gain = gain * jnp.repeat(jnp.exp(draws), shape[dim] // blocks).reshape((-1,) + (1,) * (len(shape) - 1 - dim))
    return gain


def scatter_about(key, dims, width, reach, shards=(), kind=jnp.bfloat16):
    drawn = jax.random.normal(key, dims, jnp.float32) * width
    if len(shards) > 0:
        drawn = block_levels(key, dims, shards, -0.22, 0.18) * drawn
    return jnp.clip(drawn, min=-reach, max=reach).astype(kind)


def setup_inputs(seed: int = 0) -> dict:
    key_list = jax.random.split(jax.random.key(seed), 9)
    dual_ops = draw_dual_ops(jax.random.fold_in(key_list[8], 71), 0)
    rigid_traces = scatter_about(key_list[1], (SUBDOMAINS, MODES, ORDER), (ORDER // 16) ** -0.5, 0.625, ((0, 8),), jnp.float32)
    coarse_factor = draw_coarse_factor(jax.random.fold_in(key_list[8], 71), 0)
    partner = draw_partner(jax.random.fold_in(key_list[8], 71), 0)
    send_list = draw_send_list(jax.random.fold_in(key_list[8], 71), 0)
    mode_count = touch_ends(jax.random.randint(key_list[5], (SUBDOMAINS,), 0, 7), jax.random.fold_in(key_list[5], 1), 0, 6).astype(jnp.int32)
    dual_rhs = scatter_about(key_list[6], (SUBDOMAINS, ORDER), 1.0, 6.0, ((0, 8),), jnp.float32)
    rigid_load = scatter_about(key_list[7], (COARSE,), 400.0, 2400.0, ((0, 8),), jnp.float32)
    return {"dual_ops": dual_ops, "rigid_traces": rigid_traces, "coarse_factor": coarse_factor, "partner": partner, "send_list": send_list, "mode_count": mode_count, "dual_rhs": dual_rhs, "rigid_load": rigid_load}


def reference(dual_ops, rigid_traces, coarse_factor, partner, send_list, mode_count, dual_rhs, rigid_load):
    local_blocks = SUB_DEV * BLOCKS
    codes_grid = partner.reshape(N_SUB, local_blocks)
    outgoing = send_list.reshape(N_SUB, 2, SLOTS)
    devices = jnp.arange(N_SUB, dtype=jnp.int32)[:, None]
    prev_dev = jnp.maximum(devices - 1, 0)
    next_dev = jnp.minimum(devices + 1, N_SUB - 1)
    left_slot = jnp.clip(codes_grid - local_blocks, 0, SLOTS - 1)
    right_slot = jnp.clip(codes_grid - local_blocks - SLOTS, 0, SLOTS - 1)
    from_before = prev_dev * local_blocks + jnp.maximum(outgoing[prev_dev, 1, left_slot], 0)
    from_after = next_dev * local_blocks + jnp.maximum(outgoing[next_dev, 0, right_slot], 0)
    own_block = devices * local_blocks + jnp.maximum(codes_grid, 0)
    target = jnp.where(codes_grid < local_blocks, own_block,
                       jnp.where(codes_grid < local_blocks + SLOTS, from_before, from_after)).reshape(-1)
    linked = (partner.reshape(-1) >= 0)[:, None]
    mode_mask = (jnp.arange(MODES, dtype=jnp.int32)[None, :] < mode_count[:, None]).astype(jnp.float32)

    def jump(vector):
        pieces = vector.reshape(-1, BLOCK)
        return jnp.where(linked, pieces - pieces[target], 0.0).reshape(vector.shape)

    def operator(vector):
        lowered = jump(vector).astype(jnp.bfloat16)

        def single(couple):
            return jnp.dot(couple[0], couple[1], preferred_element_type=jnp.float32)

        rows_out = lax.map(single, (dual_ops, lowered))
        return jump(rows_out)

    def restrict(vector):
        traced = jnp.einsum("skm,sm->sk", rigid_traces, jump(vector), precision=lax.Precision.HIGHEST) * mode_mask
        return traced.reshape(-1)

    def expand(coarse_vec):
        spread = jnp.einsum("skm,sk->sm", rigid_traces, coarse_vec.reshape(-1, MODES) * mode_mask,
                            precision=lax.Precision.HIGHEST)
        return jump(spread)

    def coarse(restricted):
        columns = jnp.dot(restricted, coarse_factor, precision=lax.Precision.HIGHEST)
        return jnp.dot(coarse_factor, columns, precision=lax.Precision.HIGHEST)

    def project(residual):
        projected = residual - expand(coarse(restrict(residual)))
        return projected, jnp.sum(residual * projected)

    multipliers = expand(coarse(rigid_load * mode_mask.reshape(-1)))
    residual = dual_rhs - operator(multipliers)
    projected, inner_rw = project(residual)
    direction = projected
    for turn_idx in range(ITERATIONS):
        applied = operator(direction)
        step_len = inner_rw / jnp.sum(direction * applied)
        multipliers = multipliers + step_len * direction
        residual = residual - step_len * applied
        projected, next_rw = project(residual)
        direction = projected + (next_rw / inner_rw) * direction
        inner_rw = next_rw
    return multipliers, projected
```

```python
import functools

import jax
import jax.numpy as jnp
from jax import lax
from jax.experimental import pallas as pl
from jax.experimental.pallas import tpu as pltpu
from jax.sharding import PartitionSpec as P

ITERATIONS = 2
AXES = ("sub", "crs")
LANES = 128
F32 = jnp.float32
BF16 = jnp.bfloat16


def with_halo(block, sides, width):
    for axis, dim in sides:
        count = lax.axis_size(axis)
        forward = [(i, i + 1) for i in range(count - 1)]
        backward = [(target, source) for source, target in forward]
        low = lax.ppermute(
            lax.slice_in_dim(block, block.shape[dim] - width, None, axis=dim), axis, forward
        )
        high = lax.ppermute(lax.slice_in_dim(block, 0, width, axis=dim), axis, backward)
        block = jnp.concatenate([low, block, high], axis=dim)
    return block


def plain(
    dual_ops, rigid_traces, coarse_factor, partner, send_list, mode_count, dual_rhs, rigid_load
):
    sub_count = dual_ops.shape[0]
    block_num = partner.shape[1]
    order_len = dual_ops.shape[2]
    block_len = order_len // block_num
    local_blocks = sub_count * block_num
    mode_num = rigid_traces.shape[1]
    links = partner.reshape(local_blocks)
    linked = (links >= 0)[:, None]
    source = jnp.maximum(links, 0)
    sending = (send_list >= 0)[:, :, None]
    picked = jnp.maximum(send_list, 0)
    mode_mask = (jnp.arange(mode_num, dtype=jnp.int32)[None, :] < mode_count[:, None]).astype(F32)

    def jump(vector):
        pieces = vector.reshape(local_blocks, block_len)
        parcels = jnp.where(sending, pieces[picked], 0.0)
        arrived = with_halo(parcels, (("sub", 0),), 1)
        incoming = jnp.concatenate([arrived[0], arrived[3]], axis=0)
        gathered = jnp.concatenate([pieces, incoming], axis=0)
        return jnp.where(linked, pieces - gathered[source], 0.0).reshape(vector.shape)

    def operator(vector):
        lowered = jump(vector).astype(BF16)
        partial_rows = jnp.einsum("srk,sk->sr", dual_ops, lowered, preferred_element_type=F32)
        full_rows = lax.all_gather(partial_rows, "crs", axis=1, tiled=True)
        return jump(full_rows)

    def restrict(vector):
        traced = jnp.einsum(
            "skm,sm->sk", rigid_traces, jump(vector), precision=lax.Precision.HIGHEST
        )
        return (traced * mode_mask).reshape(sub_count * mode_num)

    def expand(coarse_vec):
        scaled = coarse_vec.reshape(sub_count, mode_num) * mode_mask
        spread = jnp.einsum("skm,sk->sm", rigid_traces, scaled, precision=lax.Precision.HIGHEST)
        return jump(spread)

    def coarse(restricted, squares):
        column_part = jnp.dot(restricted, coarse_factor, precision=lax.Precision.HIGHEST)
        column_sum, total_sq = lax.psum((column_part, squares), "sub")
        back_part = jnp.dot(coarse_factor, column_sum, precision=lax.Precision.HIGHEST)
        solved, folded = lax.psum((back_part, jnp.sum(column_sum * column_sum)), "crs")
        return (solved, total_sq, folded)

    def project(residual):
        solved, total_sq, folded = coarse(restrict(residual), jnp.sum(residual * residual))
        return (residual - expand(solved), total_sq - folded)

    start_load = rigid_load * mode_mask.reshape(sub_count * mode_num)
    start_solved, _, _ = coarse(start_load, jnp.zeros((), F32))
    multipliers = expand(start_solved)
    residual = dual_rhs - operator(multipliers)
    projected, inner_rw = project(residual)
    direction = projected
    for _ in range(ITERATIONS):
        applied = operator(direction)
        curvature = lax.psum(jnp.sum(direction * applied), "sub")
        step_len = inner_rw / curvature
        multipliers = multipliers + step_len * direction
        residual = residual - step_len * applied
        projected, next_rw = project(residual)
        direction = projected + next_rw / inner_rw * direction
        inner_rw = next_rw
    return (multipliers, projected)


def split3(value):
    high = value.astype(BF16)
    rest = value - high.astype(F32)
    mid = rest.astype(BF16)
    low = (rest - mid.astype(F32)).astype(BF16)
    return high, mid, low


def select_dot(chooser, value):
    width = value.shape[1]
    wide = jnp.dot(
        chooser, jnp.concatenate(split3(value), axis=1), preferred_element_type=F32
    )
    return (wide[:, 2 * width :] + wide[:, width : 2 * width]) + wide[:, :width]


def one_hot(column, width):
    rows = column.shape[0]
    return (lax.broadcasted_iota(jnp.int32, (rows, width), 1) == column).astype(F32)


def total(value):
    return jnp.sum(jnp.sum(value, axis=0, keepdims=True), axis=1, keepdims=True)


class Shape:
    def __init__(self, dual_ops, rigid_traces, coarse_factor, partner, send_list):
        self.subs, self.rows, self.order = dual_ops.shape
        self.blocks = partner.shape[1]
        self.modes = rigid_traces.shape[1]
        self.slots = send_list.shape[1]
        self.crs = lax.axis_size("crs")
        self.ndev = lax.axis_size("sub") * self.crs
        self.pad = -(-self.subs // 16) * 16
        self.all_rows = self.blocks * self.pad
        self.piece_blocks = self.rows // LANES
        self.piece = self.piece_blocks * self.pad
        self.cols = coarse_factor.shape[1]
        self.halves = -(-(self.cols + 8) // LANES)
        self.wide = self.halves * LANES
        self.t_rows = self.crs * self.halves
        self.spot = self.cols - (self.halves - 1) * LANES

    def scalar_at(self, index):
        rows = lax.broadcasted_iota(jnp.int32, (self.t_rows, LANES), 0)
        lanes = lax.broadcasted_iota(jnp.int32, (self.t_rows, LANES), 1)
        return (rows == self.halves - 1) & (lanes == self.spot + index)

    def t_mask(self):
        rows = lax.broadcasted_iota(jnp.int32, (self.t_rows, LANES), 0)
        lanes = lax.broadcasted_iota(jnp.int32, (self.t_rows, LANES), 1)
        return (rows % self.halves < self.halves - 1) | (lanes < self.spot)

    def slot_of(self, rel):
        return (rel % 2) * (self.crs // 2) + rel // 2


def rows_of(value, sh):
    return jnp.concatenate(
        [value[:, b * LANES : (b + 1) * LANES] for b in range(value.shape[1] // LANES)], axis=0
    )


def lanes_of(value, sh):
    return jnp.concatenate(
        [value[b * sh.pad : (b + 1) * sh.pad] for b in range(value.shape[0] // sh.pad)], axis=1
    )


def factor_tile(w_refs, sh, rel, where, mode):
    slot = sh.slot_of(rel)
    half = sh.crs // 2
    ref = w_refs[slot // half]
    base = ((slot % half) * 3 + where) * sh.modes * sh.pad + mode * sh.pad
    return ref[base : base + sh.pad, :]


def coarse_back(w_refs, t_ref, me, sh):
    t_row = []
    for rel in range(sh.crs):
        at = jnp.bitwise_xor(me, rel) * sh.halves
        t_row.append(
            jnp.concatenate([t_ref[pl.ds(at + h, 1), :] for h in range(sh.halves)], axis=1)
        )
    columns = []
    for mode in range(sh.modes):
        parts = []
        for where in range(3):
            acc = jnp.zeros((sh.pad, sh.wide), F32)
            for rel in range(sh.crs):
                acc += factor_tile(w_refs, sh, rel, where, mode) * t_row[rel]
            parts.append(
                jnp.broadcast_to(jnp.sum(acc, axis=1, keepdims=True), (sh.pad, LANES))
            )
        columns.append(jnp.concatenate(parts, axis=0))
    return jnp.concatenate(columns, axis=1)


def lift(tr_ref, pt_ref, ep_ref, w_refs, t_ref, me, sh):
    spread = coarse_back(w_refs, t_ref, me, sh)
    far = select_dot(ep_ref[...], spread)
    out = jnp.zeros((sh.all_rows, LANES), F32)
    for mode in range(sh.modes):
        own = spread[: sh.pad, mode * LANES : (mode + 1) * LANES]
        own = jnp.concatenate([own] * sh.blocks, axis=0)
        out += tr_ref[mode] * own - pt_ref[mode] * far[:, mode * LANES : (mode + 1) * LANES]
    return out


def coarse_part(value, tr_ref, pt_ref, ept_ref, w_refs, me, sh, t_out):
    at = pl.multiple_of(me * sh.piece, 16)
    own, far = [], []
    for mode in range(sh.modes):
        mine = tr_ref[mode, pl.ds(at, sh.piece), :] * value
        acc = mine[: sh.pad]
        for b in range(1, sh.piece_blocks):
            acc = acc + mine[b * sh.pad : (b + 1) * sh.pad]
        own.append(acc)
        far.append(pt_ref[mode, pl.ds(at, sh.piece), :] * value)
    moved = select_dot(ept_ref[...], jnp.concatenate(far, axis=1))
    sums = [jnp.zeros((sh.pad, sh.wide), F32) for _ in range(sh.crs)]
    for mode in range(sh.modes):
        moved_k = moved[:, mode * LANES : (mode + 1) * LANES]
        for where in range(3):
            part = -moved_k[where * sh.pad : (where + 1) * sh.pad]
            if where == 0:
                part = part + own[mode]
            weight = jnp.sum(part, axis=1, keepdims=True)
            for rel in range(sh.crs):
                sums[rel] = sums[rel] + factor_tile(w_refs, sh, rel, where, mode) * weight
    for rel in range(sh.crs):
        row = jnp.sum(sums[rel], axis=0, keepdims=True)
        at_t = jnp.bitwise_xor(me, rel) * sh.halves
        for h in range(sh.halves):
            t_out[pl.ds(at_t + h, 1), :] = row[:, h * LANES : (h + 1) * LANES]


def start_ops(ops_hbm, ops_vmem, sems, sh):
    for s in range(sh.subs):
        pltpu.make_async_copy(ops_hbm.at[s], ops_vmem.at[s], sems.at[s]).start()


def product(lowered, ops_hbm, ops_vmem, sems, sh):
    row = lax.broadcasted_iota(jnp.int32, (sh.pad, sh.rows), 0)
    acc = jnp.zeros((sh.pad, sh.rows), F32)
    for s in range(sh.subs):
        pltpu.make_async_copy(ops_hbm.at[s], ops_vmem.at[s], sems.at[s]).wait()
        part = lax.dot_general(
            lowered, ops_vmem[s], (((1,), (1,)), ((), ())), preferred_element_type=F32
        )
        acc = jnp.where(row == s, part, acc)
    return rows_of(acc, sh)


def sum_parcels(t_in_ref, sh):
    acc = t_in_ref[0]
    for i in range(1, sh.ndev):
        acc = acc + t_in_ref[i]
    return acc


def pick(t_sum, sh, index):
    return total(jnp.where(sh.scalar_at(index), t_sum, 0.0))


def norm2(t_vec, sh):
    return total(jnp.where(sh.t_mask(), t_vec * t_vec, 0.0))


def send_t(t_scr, scalars, sh, t_out):
    payload = jnp.where(sh.t_mask(), t_scr[...], 0.0)
    for index, value in scalars.items():
        payload = jnp.where(sh.scalar_at(index), value, payload)
    if len(t_out.shape) == 2:
        t_out[...] = payload
    else:
        for i in range(sh.ndev):
            t_out[i] = payload


def pack_kernel(sh, me_ref, tr_ref, send_ref, load_ref, factor_ref, parcel_a, parcel_b, t_out):
    for which, out in ((0, parcel_a), (1, parcel_b)):
        chooser = one_hot(send_ref[:, which : which + 1], sh.all_rows).astype(BF16)
        for k in range(sh.modes + 1):
            out[k] = select_dot(chooser, tr_ref[k])
    part = jnp.dot(
        load_ref[...], factor_ref[...], preferred_element_type=F32, precision=lax.Precision.HIGHEST
    )
    part = jnp.concatenate(
        [part, jnp.zeros((part.shape[0], sh.wide - sh.cols), F32)], axis=1
    )[:1]
    rows = lax.broadcasted_iota(jnp.int32, (sh.t_rows, LANES), 0)
    payload = jnp.zeros((sh.t_rows, LANES), F32)
    for h in range(sh.halves):
        payload = jnp.where(
            rows == me_ref[0] * sh.halves + h, part[:, h * LANES : (h + 1) * LANES], payload
        )
    for i in range(sh.ndev):
        t_out[i] = payload


def first_kernel(
    sh, me_ref, tr_in, halo_a, halo_b, index_ref, psub_ref, t_in, w0, w1, ops_hbm,
    tr_out, pt_out, jump_out, ep_out, ept_out, lam_out, q_out, t_out,
    t_scr, ops_vmem, sems,
):
    start_ops(ops_hbm, ops_vmem, sems, sh)
    me = me_ref[0]
    w_refs = (w0, w1)
    index = index_ref[...]
    live = (index[:, 2:3] >= 0).astype(F32)
    col_num = 3 * sh.crs * sh.piece
    jump_out[...] = (one_hot(index[:, 0:1], col_num) - one_hot(index[:, 1:2], col_num)).astype(BF16)
    ep_out[...] = one_hot(index[:, 3:4], 3 * sh.pad).astype(BF16)
    ept_out[...] = (
        lax.broadcasted_iota(jnp.int32, (3 * sh.pad, sh.piece), 0) == psub_ref[...]
    ).astype(BF16)
    source = one_hot(index[:, 2:3], sh.all_rows + 2 * sh.slots).astype(BF16)
    for k in range(sh.modes + 1):
        whole = jnp.concatenate([tr_in[k], halo_a[k], halo_b[k]], axis=0)
        far = select_dot(source, whole)
        if k < sh.modes:
            tr_out[k] = tr_in[k] * live
            pt_out[k] = far
        else:
            tr_out[k] = tr_in[k]
            pt_out[k] = tr_in[k] * live - far
    t_scr[...] = sum_parcels(t_in, sh)
    lam = lift(tr_out, pt_out, ep_out, w_refs, t_scr, me, sh)
    lam_out[...] = lam
    lowered = lanes_of(2.0 * lam, sh).astype(BF16)
    q = product(lowered, ops_hbm, ops_vmem, sems, sh)
    q_out[...] = q
    at = pl.multiple_of(me * sh.piece, 16)
    value = tr_out[sh.modes, pl.ds(at, sh.piece), :] - 2.0 * q
    coarse_part(value, tr_out, pt_out, ept_out, w_refs, me, sh, t_scr)
    send_t(t_scr, {}, sh, t_out)


def second_kernel(
    sh, me_ref, tr_ref, pt_ref, jump_ref, ep_ref, ept_ref, q0, q1, t_in, w0, w1, ops_hbm,
    r_out, jr_out, d_out, jd_out, tr0_out, q_out, t_out,
    t_scr, ops_vmem, sems,
):
    start_ops(ops_hbm, ops_vmem, sems, sh)
    me = me_ref[0]
    w_refs = (w0, w1)
    tr0_out[...] = sum_parcels(t_in, sh)
    applied = select_dot(jump_ref[...], jnp.concatenate([q0[...], q1[...]], axis=0))
    back = lift(tr_ref, pt_ref, ep_ref, w_refs, tr0_out, me, sh)
    residual = tr_ref[sh.modes] - applied
    r_out[...] = residual
    jump_r = pt_ref[sh.modes] - 2.0 * applied
    jr_out[...] = jump_r
    d_out[...] = residual - back
    jump_d = jump_r - 2.0 * back
    jd_out[...] = jump_d
    q = product(lanes_of(jump_d, sh).astype(BF16), ops_hbm, ops_vmem, sems, sh)
    q_out[...] = q
    coarse_part(2.0 * q, tr_ref, pt_ref, ept_ref, w_refs, me, sh, t_scr)
    at = pl.multiple_of(me * sh.piece, 16)
    mine = pl.ds(at, sh.piece)
    send_t(
        t_scr,
        {
            0: total(jd_out[mine, :] * q),
            1: total(jr_out[mine, :] * q),
            2: total(r_out[mine, :] * r_out[mine, :]),
        },
        sh,
        t_out,
    )


def square_kernel(sh, me_ref, jump_ref, q0, q1, t_in, applied_out, t_out):
    me = me_ref[0]
    applied_out[...] = select_dot(jump_ref[...], jnp.concatenate([q0[...], q1[...]], axis=0))
    at = pl.multiple_of(me * sh.piece, 16)
    mine = applied_out[pl.ds(at, sh.piece), :]
    payload = jnp.where(sh.scalar_at(3), total(mine * mine), t_in[...])
    for i in range(sh.ndev):
        t_out[i] = payload


def third_kernel(
    sh, me_ref, tr_ref, pt_ref, ep_ref, ept_ref, applied_ref, t_in, w0, w1, r_ref, jr_ref, d_ref,
    jd_ref, tr0_ref, lam_ref, ops_hbm,
    r_out, d_out, lam_out, tr1_out, q_out, t_out,
    t_scr, jd_scr, ops_vmem, sems,
):
    start_ops(ops_hbm, ops_vmem, sems, sh)
    me = me_ref[0]
    w_refs = (w0, w1)
    sums = sum_parcels(t_in, sh)
    tr0 = tr0_ref[...]
    d_a, r_a, r_r, a_a = (pick(sums, sh, i) for i in range(4))
    rw0 = r_r - norm2(tr0, sh)
    alpha = rw0 / d_a
    tr1 = tr0 - alpha * sums
    rw1 = (r_r - 2.0 * alpha * r_a + alpha * alpha * a_a) - norm2(tr1, sh)
    beta = rw1 / rw0
    tr1_out[...] = jnp.where(sh.scalar_at(0), rw1, tr1)
    back = lift(tr_ref, pt_ref, ep_ref, w_refs, tr1_out, me, sh)
    applied = applied_ref[...]
    residual = r_ref[...] - alpha * applied
    r_out[...] = residual
    lam_out[...] = lam_ref[...] + alpha * d_ref[...]
    d_out[...] = (residual - back) + beta * d_ref[...]
    jump_d = (jr_ref[...] - 2.0 * alpha * applied - 2.0 * back) + beta * jd_ref[...]
    jd_scr[...] = jump_d
    q = product(lanes_of(jump_d, sh).astype(BF16), ops_hbm, ops_vmem, sems, sh)
    q_out[...] = q
    coarse_part(2.0 * q, tr_ref, pt_ref, ept_ref, w_refs, me, sh, t_scr)
    at = pl.multiple_of(me * sh.piece, 16)
    send_t(t_scr, {0: total(jd_scr[pl.ds(at, sh.piece), :] * q)}, sh, t_out)


def last_kernel(
    sh, me_ref, tr_ref, pt_ref, jump_ref, ep_ref, q0, q1, t_in, w0, w1, r_ref, d_ref, lam_ref,
    tr1_ref, lam_out, p_out, t_scr,
):
    me = me_ref[0]
    sums = sum_parcels(t_in, sh)
    tr1 = tr1_ref[...]
    alpha = pick(tr1, sh, 0) / pick(sums, sh, 0)
    t_scr[...] = tr1 - alpha * sums
    applied = select_dot(jump_ref[...], jnp.concatenate([q0[...], q1[...]], axis=0))
    back = lift(tr_ref, pt_ref, ep_ref, (w0, w1), t_scr, me, sh)
    lam = lam_ref[...] + alpha * d_ref[...]
    projected = (r_ref[...] - alpha * applied) - back
    lam_out[...] = lanes_of(lam, sh)[: sh.subs]
    p_out[...] = lanes_of(projected, sh)[: sh.subs]


def permute(value, move):
    sub_num, crs_num = lax.axis_size("sub"), lax.axis_size("crs")
    pairs = []
    for i in range(sub_num):
        for j in range(crs_num):
            to_i, to_j = move(i, j)
            if 0 <= to_i < sub_num:
                pairs.append((i * crs_num + j, to_i * crs_num + to_j))
    return lax.ppermute(value, AXES, pairs)


def swap_a(value):
    return permute(value, lambda i, j: (i ^ 1, j))


def swap_b(value):
    return permute(value, lambda i, j: (((i + 1) ^ 1) - 1, j))


def spread_pieces(value):
    crs_num = lax.axis_size("crs")
    near = jnp.concatenate([value, swap_a(value), swap_b(value)], axis=0)
    group = [near]
    for shift in range(1, crs_num // 2):
        group.append(permute(near, lambda i, j: (i, j ^ (2 * shift))))
    first = jnp.concatenate(group, axis=0)
    return first, permute(first, lambda i, j: (i, j ^ 1))


def local(
    dual_ops, rigid_traces, coarse_factor, partner, send_list, mode_count, dual_rhs, rigid_load
):
    sh = Shape(dual_ops, rigid_traces, coarse_factor, partner, send_list)
    me = lax.axis_index("crs")
    odd = lax.axis_index("sub") % 2
    blocks, pad, subs, modes = sh.blocks, sh.pad, sh.subs, sh.modes
    local_blocks = subs * blocks
    extra = pad - subs

    mode_mask = (jnp.arange(modes, dtype=jnp.int32)[None, :] < mode_count[:, None]).astype(F32)
    fields = jnp.concatenate([rigid_traces * mode_mask[:, :, None], dual_rhs[:, None, :]], axis=1)
    fields = fields.reshape(subs, modes + 1, blocks, LANES).transpose(1, 2, 0, 3)
    fields = jnp.pad(fields, ((0, 0), (0, 0), (0, extra), (0, 0)))
    fields = fields.reshape(modes + 1, sh.all_rows, LANES)
    load = jnp.broadcast_to((rigid_load * mode_mask.reshape(-1))[None, :], (8, subs * modes))

    factor = coarse_factor.reshape(subs, modes, sh.cols).transpose(1, 0, 2)
    factor = jnp.pad(factor, ((0, 0), (0, extra), (0, sh.wide - sh.cols)))
    factor = factor.reshape(modes * pad, sh.wide)

    to_a = jnp.where(odd == 1, send_list[0], send_list[1])
    to_b = jnp.where(odd == 1, send_list[1], send_list[0])
    from_a, from_b = swap_a(to_a), swap_b(to_b)
    outgoing = jnp.stack([to_a, to_b], axis=1)
    outgoing = jnp.where(outgoing >= 0, (outgoing % blocks) * pad + outgoing // blocks, -1)

    code = jnp.pad(partner.T, ((0, 0), (0, extra)), constant_values=-1).reshape(sh.all_rows)
    own_row = jnp.arange(sh.all_rows, dtype=jnp.int32)
    is_own = (code >= 0) & (code < local_blocks)
    before = (code >= local_blocks) & (code < local_blocks + sh.slots)
    slot = jnp.where(before, code - local_blocks, code - local_blocks - sh.slots)
    is_a = (code >= local_blocks) & (before == (odd == 1))
    is_b = (code >= local_blocks) & (before != (odd == 1))
    hit = slot[:, None] == jnp.arange(sh.slots, dtype=jnp.int32)[None, :]
    theirs = jnp.where(is_a[:, None], from_a[None, :], from_b[None, :])
    theirs = jnp.sum(jnp.where(hit, theirs, 0), axis=1)
    there = jnp.where(is_own, code, theirs)
    there_s, there_b = there // blocks, there % blocks
    where_d = jnp.where(is_own, 0, jnp.where(is_a, 1, 2))

    def piece_row(block, sub, where):
        place = sh.slot_of(jnp.bitwise_xor(block // sh.piece_blocks, me)) * 3 + where
        return place * sh.piece + (block % sh.piece_blocks) * pad + sub

    linked = code >= 0
    own_col = jnp.where(linked, piece_row(own_row // pad, own_row % pad, 0), -1)
    far_col = jnp.where(linked, piece_row(there_b, there_s, where_d), -1)
    trace_col = jnp.where(
        is_own,
        there_b * pad + there_s,
        jnp.where(is_a, sh.all_rows + slot, sh.all_rows + sh.slots + slot),
    )
    trace_col = jnp.where(linked, trace_col, -1)
    far_sub = jnp.where(linked, where_d * pad + there_s, -1)
    index = jnp.stack([own_col, far_col, trace_col, far_sub], axis=1)
    piece_sub = lax.dynamic_slice_in_dim(far_sub, me * sh.piece, sh.piece)[None, :]
    me_arr = me.reshape(1)

    vmem = pl.BlockSpec(memory_space=pltpu.VMEM)
    smem = pl.BlockSpec(memory_space=pltpu.SMEM)
    hbm = pl.BlockSpec(memory_space=pl.ANY)
    params = pltpu.CompilerParams(vmem_limit_bytes=48 * 1024 * 1024)

    def call(kernel, outs, scratch, *operands, name):
        ops = any(x is dual_ops for x in operands)
        if ops:
            scratch = scratch + [
                pltpu.VMEM(dual_ops.shape, BF16),
                pltpu.SemaphoreType.DMA((subs,)),
            ]
        return pl.pallas_call(
            functools.partial(kernel, sh),
            out_shape=[jax.ShapeDtypeStruct(s, t) for s, t in outs],
            in_specs=[smem] + [hbm if x is dual_ops else vmem for x in operands],
            out_specs=[vmem] * len(outs),
            scratch_shapes=scratch,
            compiler_params=params,
            name=name,
        )(me_arr, *operands)

    state = ((sh.all_rows, LANES), F32)
    t_shape = ((sh.t_rows, LANES), F32)
    parcels = ((sh.ndev, sh.t_rows, LANES), F32)
    q_shape = ((sh.piece, LANES), F32)
    field_shape = (fields.shape, F32)
    t_scratch = [pltpu.VMEM((sh.t_rows, LANES), F32)]

    def exchange(parcel):
        return lax.all_to_all(parcel, AXES, 0, 0)

    parcel_shape = ((modes + 1, sh.slots, LANES), F32)
    parcel_a, parcel_b, t_part = call(
        pack_kernel, [parcel_shape, parcel_shape, parcels], [],
        fields, outgoing, load, coarse_factor, name="pack",
    )
    halo_a, halo_b = swap_a(parcel_a), swap_b(parcel_b)
    w0, w1 = spread_pieces(factor)
    t_in = exchange(t_part)

    traces, far_traces, jumper, far_pick, far_put, lam0, q, t_part = call(
        first_kernel,
        [
            field_shape, field_shape,
            ((sh.all_rows, 3 * sh.crs * sh.piece), BF16),
            ((sh.all_rows, 3 * pad), BF16),
            ((3 * pad, sh.piece), BF16),
            state, q_shape, parcels,
        ],
        t_scratch,
        fields, halo_a, halo_b, index, piece_sub, t_in, w0, w1, dual_ops, name="first",
    )
    q0, q1 = spread_pieces(q)
    t_in = exchange(t_part)

    r0, jr0, d0, jd0, tr0, q, t_part = call(
        second_kernel,
        [state, state, state, state, t_shape, q_shape, t_shape],
        t_scratch,
        traces, far_traces, jumper, far_pick, far_put, q0, q1, t_in, w0, w1, dual_ops,
        name="second",
    )
    q0, q1 = spread_pieces(q)
    applied, t_part = call(
        square_kernel, [state, parcels], [], jumper, q0, q1, t_part, name="square"
    )
    t_in = exchange(t_part)

    r1, d1, lam1, tr1, q, t_part = call(
        third_kernel,
        [state, state, state, t_shape, q_shape, parcels],
        t_scratch + [pltpu.VMEM((sh.all_rows, LANES), F32)],
        traces, far_traces, far_pick, far_put, applied, t_in, w0, w1, r0, jr0, d0, jd0, tr0, lam0,
        dual_ops, name="third",
    )
    q0, q1 = spread_pieces(q)
    t_in = exchange(t_part)

    multipliers, projected = call(
        last_kernel,
        [((subs, sh.order), F32), ((subs, sh.order), F32)],
        t_scratch,
        traces, far_traces, jumper, far_pick, q0, q1, t_in, w0, w1, r1, d1, lam1, tr1,
        name="last",
    )
    return multipliers, projected


def body(*args):
    dual_ops, _, _, partner = args[:4]
    crs_num, sub_num = lax.axis_size("crs"), lax.axis_size("sub")
    whole_blocks = (
        dual_ops.shape[2] // partner.shape[1] == LANES and dual_ops.shape[1] % LANES == 0
    )
    if whole_blocks and crs_num % 2 == 0 and crs_num & (crs_num - 1) == 0 and sub_num % 2 == 0:
        return local(*args)
    return plain(*args)


def solution(mesh):
    return jax.shard_map(
        body,
        mesh=mesh,
        in_specs=(
            P("sub", "crs", None),
            P("sub", None, None),
            P("sub", "crs"),
            P("sub", None),
            P("sub", None),
            P("sub"),
            P("sub", None),
            P("sub"),
        ),
        out_specs=(P("sub", None), P("sub", None)),
        check_vma=False,
    )
```

```python
import functools

import jax
import jax.numpy as jnp
from jax import lax
from jax.experimental import pallas as pl
from jax.experimental.pallas import tpu as pltpu
from jax.sharding import PartitionSpec as P

ITERATIONS = 2
AXES = ("sub", "crs")
LANES = 128
F32 = jnp.float32
BF16 = jnp.bfloat16


def with_halo(block, sides, width):
    for axis, dim in sides:
        count = lax.axis_size(axis)
        forward = [(i, i + 1) for i in range(count - 1)]
        backward = [(target, source) for source, target in forward]
        low = lax.ppermute(
            lax.slice_in_dim(block, block.shape[dim] - width, None, axis=dim), axis, forward
        )
        high = lax.ppermute(lax.slice_in_dim(block, 0, width, axis=dim), axis, backward)
        block = jnp.concatenate([low, block, high], axis=dim)
    return block


def plain(
    dual_ops, rigid_traces, coarse_factor, partner, send_list, mode_count, dual_rhs, rigid_load
):
    sub_count = dual_ops.shape[0]
    block_num = partner.shape[1]
    order_len = dual_ops.shape[2]
    block_len = order_len // block_num
    local_blocks = sub_count * block_num
    mode_num = rigid_traces.shape[1]
    links = partner.reshape(local_blocks)
    linked = (links >= 0)[:, None]
    source = jnp.maximum(links, 0)
    sending = (send_list >= 0)[:, :, None]
    picked = jnp.maximum(send_list, 0)
    mode_mask = (jnp.arange(mode_num, dtype=jnp.int32)[None, :] < mode_count[:, None]).astype(F32)

    def jump(vector):
        pieces = vector.reshape(local_blocks, block_len)
        parcels = jnp.where(sending, pieces[picked], 0.0)
        arrived = with_halo(parcels, (("sub", 0),), 1)
        incoming = jnp.concatenate([arrived[0], arrived[3]], axis=0)
        gathered = jnp.concatenate([pieces, incoming], axis=0)
        return jnp.where(linked, pieces - gathered[source], 0.0).reshape(vector.shape)

    def operator(vector):
        lowered = jump(vector).astype(BF16)
        partial_rows = jnp.einsum("srk,sk->sr", dual_ops, lowered, preferred_element_type=F32)
        full_rows = lax.all_gather(partial_rows, "crs", axis=1, tiled=True)
        return jump(full_rows)

    def restrict(vector):
        traced = jnp.einsum(
            "skm,sm->sk", rigid_traces, jump(vector), precision=lax.Precision.HIGHEST
        )
        return (traced * mode_mask).reshape(sub_count * mode_num)

    def expand(coarse_vec):
        scaled = coarse_vec.reshape(sub_count, mode_num) * mode_mask
        spread = jnp.einsum("skm,sk->sm", rigid_traces, scaled, precision=lax.Precision.HIGHEST)
        return jump(spread)

    def coarse(restricted, squares):
        column_part = jnp.dot(restricted, coarse_factor, precision=lax.Precision.HIGHEST)
        column_sum, total_sq = lax.psum((column_part, squares), "sub")
        back_part = jnp.dot(coarse_factor, column_sum, precision=lax.Precision.HIGHEST)
        solved, folded = lax.psum((back_part, jnp.sum(column_sum * column_sum)), "crs")
        return (solved, total_sq, folded)

    def project(residual):
        solved, total_sq, folded = coarse(restrict(residual), jnp.sum(residual * residual))
        return (residual - expand(solved), total_sq - folded)

    start_load = rigid_load * mode_mask.reshape(sub_count * mode_num)
    start_solved, _, _ = coarse(start_load, jnp.zeros((), F32))
    multipliers = expand(start_solved)
    residual = dual_rhs - operator(multipliers)
    projected, inner_rw = project(residual)
    direction = projected
    for _ in range(ITERATIONS):
        applied = operator(direction)
        curvature = lax.psum(jnp.sum(direction * applied), "sub")
        step_len = inner_rw / curvature
        multipliers = multipliers + step_len * direction
        residual = residual - step_len * applied
        projected, next_rw = project(residual)
        direction = projected + next_rw / inner_rw * direction
        inner_rw = next_rw
    return (multipliers, projected)


def split3(value):
    high = value.astype(BF16)
    rest = value - high.astype(F32)
    mid = rest.astype(BF16)
    low = (rest - mid.astype(F32)).astype(BF16)
    return high, mid, low


def select_dot(chooser, value):
    width = value.shape[1]
    wide = jnp.dot(
        chooser, jnp.concatenate(split3(value), axis=1), preferred_element_type=F32
    )
    return (wide[:, 2 * width :] + wide[:, width : 2 * width]) + wide[:, :width]


def one_hot(column, width):
    rows = column.shape[0]
    return (lax.broadcasted_iota(jnp.int32, (rows, width), 1) == column).astype(F32)


def repeated_one_hot(code, width):
    lane = lax.broadcasted_iota(jnp.int32, code.shape, 1)
    tiles = [(lane + at == code).astype(F32) for at in range(0, width, LANES)]
    return jnp.concatenate(tiles, axis=1)[:, :width].astype(BF16)


def floor_div(value, by, most):
    out = jnp.zeros(value.shape, jnp.int32)
    for i in range(1, most):
        out = out + (value >= i * by).astype(jnp.int32)
    return out


def total(value):
    return jnp.sum(jnp.sum(value, axis=0, keepdims=True), axis=1, keepdims=True)


class Shape:
    def __init__(self, dual_ops, rigid_traces, coarse_factor, partner, send_list):
        self.subs, self.rows, self.order = dual_ops.shape
        self.blocks = partner.shape[1]
        self.modes = rigid_traces.shape[1]
        self.slots = send_list.shape[1]
        self.crs = lax.axis_size("crs")
        self.ndev = lax.axis_size("sub") * self.crs
        self.pad = -(-self.subs // 16) * 16
        self.all_rows = self.blocks * self.pad
        self.piece_blocks = self.rows // LANES
        self.piece = self.piece_blocks * self.pad
        self.half_slots = -(-self.slots // 16) * 8
        self.planes = self.modes + 1
        self.group = 2 if self.subs % 2 == 0 else 1
        self.names_at = self.planes * self.half_slots
        self.slot_lanes = -(-2 * self.half_slots // LANES) * LANES
        self.parcel = self.names_at + 8 * (self.slot_lanes // LANES)
        self.cols = coarse_factor.shape[1]
        self.full = self.cols // LANES
        self.spot = self.cols % LANES
        self.halves = self.full + 1
        self.wide = self.halves * LANES
        self.t_rows = self.crs * self.halves
        self.tile_rows = self.modes * self.pad
        self.beside = LANES // max(self.spot, 1)
        self.rest_tiles = -(-self.modes // self.beside) if self.spot else 0
        self.factor_rows = self.full * self.tile_rows + self.rest_tiles * self.pad

    def scalar_at(self, index):
        rows = lax.broadcasted_iota(jnp.int32, (self.t_rows, LANES), 0)
        lanes = lax.broadcasted_iota(jnp.int32, (self.t_rows, LANES), 1)
        return (rows == self.halves - 1) & (lanes == self.spot + index)

    def t_mask(self):
        rows = lax.broadcasted_iota(jnp.int32, (self.t_rows, LANES), 0)
        lanes = lax.broadcasted_iota(jnp.int32, (self.t_rows, LANES), 1)
        return (rows % self.halves < self.halves - 1) | (lanes < self.spot)

    def slot_of(self, rel):
        return (rel % 2) * (self.crs // 2) + rel // 2


def rows_of(value, sh):
    return jnp.concatenate(
        [value[:, b * LANES : (b + 1) * LANES] for b in range(value.shape[1] // LANES)], axis=0
    )


def rows_of_lanes(value):
    return jnp.concatenate(
        [value[:, at : at + LANES] for at in range(0, value.shape[1], LANES)], axis=0
    )


def lanes_of(value, sh):
    return jnp.concatenate(
        [value[b * sh.pad : (b + 1) * sh.pad] for b in range(value.shape[0] // sh.pad)], axis=1
    )


def factor_tile(w_refs, sh, rel, where, at):
    slot = sh.slot_of(rel)
    xs = sh.crs // 2
    base = ((slot % xs) * 3 + where) * sh.factor_rows + at
    return w_refs[slot // xs][base : base + sh.pad, :]


def full_tile(w_refs, sh, rel, where, mode, h):
    return factor_tile(w_refs, sh, rel, where, h * sh.tile_rows + mode * sh.pad)


def rest_tile(w_refs, sh, rel, where, tile):
    return factor_tile(w_refs, sh, rel, where, sh.full * sh.tile_rows + tile * sh.pad)


def lane_group(sh, shape):
    lane = lax.broadcasted_iota(jnp.int32, shape, 1)
    return floor_div(lane, sh.spot, sh.beside + 1)


def coarse_back(w_refs, t_ref, me, sh):
    t_row, t_rest = {}, []
    lane = lax.broadcasted_iota(jnp.int32, (8, LANES), 1)
    for rel in range(sh.crs):
        at = jnp.bitwise_xor(me, rel) * sh.halves
        for h in range(sh.full):
            t_row[rel, h] = t_ref[pl.ds(at + h, 1), :]
        if sh.spot:
            rest = jnp.broadcast_to(t_ref[pl.ds(at + sh.full, 1), :], (8, LANES))
            rest = jnp.where(lane < sh.spot, rest, 0.0)
            spread = rest
            for i in range(1, sh.beside):
                spread = spread + pltpu.roll(rest, i * sh.spot, 1)
            t_rest.append(spread[:1])
    rests = {}
    for where in range(3):
        for tile in range(sh.rest_tiles):
            acc = jnp.zeros((sh.pad, LANES), F32)
            for rel in range(sh.crs):
                acc += rest_tile(w_refs, sh, rel, where, tile) * t_rest[rel]
            rests[where, tile] = acc
    group = lane_group(sh, (sh.pad, LANES)) if sh.spot else None
    columns = []
    for mode in range(sh.modes):
        parts = []
        for where in range(3):
            acc = jnp.zeros((sh.pad, LANES), F32)
            if sh.spot:
                mine = group == mode % sh.beside
                acc = jnp.where(mine, rests[where, mode // sh.beside], 0.0)
            for rel in range(sh.crs):
                for h in range(sh.full):
                    acc += full_tile(w_refs, sh, rel, where, mode, h) * t_row[rel, h]
            parts.append(
                jnp.broadcast_to(jnp.sum(acc, axis=1, keepdims=True), (sh.pad, LANES))
            )
        columns.append(jnp.concatenate(parts, axis=0))
    return jnp.concatenate(columns, axis=1)


def lift(tr_ref, pt_ref, ep_ref, w_refs, t_ref, me, sh):
    spread = coarse_back(w_refs, t_ref, me, sh)
    far = select_dot(ep_ref[...], spread)
    out = jnp.zeros((sh.all_rows, LANES), F32)
    for mode in range(sh.modes):
        own = spread[: sh.pad, mode * LANES : (mode + 1) * LANES]
        own = jnp.concatenate([own] * sh.blocks, axis=0)
        out += tr_ref[mode] * own - pt_ref[mode] * far[:, mode * LANES : (mode + 1) * LANES]
    return out


def coarse_part(value, tr_ref, pt_ref, ept_ref, w_refs, me, sh, t_out):
    at = pl.multiple_of(me * sh.piece, 16)
    own, far = [], []
    for mode in range(sh.modes):
        mine = tr_ref[mode, pl.ds(at, sh.piece), :] * value
        acc = mine[: sh.pad]
        for b in range(1, sh.piece_blocks):
            acc = acc + mine[b * sh.pad : (b + 1) * sh.pad]
        own.append(acc)
        far.append(pt_ref[mode, pl.ds(at, sh.piece), :] * value)
    moved = select_dot(ept_ref[...], jnp.concatenate(far, axis=1))
    sums, rests = {}, {}
    group = lane_group(sh, (sh.pad, LANES)) if sh.spot else None
    side = {}

    def add(table, key, term):
        table[key] = table[key] + term if key in table else term

    for mode in range(sh.modes):
        moved_k = moved[:, mode * LANES : (mode + 1) * LANES]
        for where in range(3):
            part = -moved_k[where * sh.pad : (where + 1) * sh.pad]
            if where == 0:
                part = part + own[mode]
            weight = jnp.broadcast_to(jnp.sum(part, axis=1, keepdims=True), (sh.pad, LANES))
            for rel in range(sh.crs):
                for h in range(sh.full):
                    add(sums, (rel, h), full_tile(w_refs, sh, rel, where, mode, h) * weight)
            if sh.spot:
                mine = group == mode % sh.beside
                add(side, (where, mode // sh.beside), jnp.where(mine, weight, 0.0))
    for (where, tile), weight in side.items():
        for rel in range(sh.crs):
            add(rests, rel, rest_tile(w_refs, sh, rel, where, tile) * weight)
    for rel in range(sh.crs):
        at_t = jnp.bitwise_xor(me, rel) * sh.halves
        for h in range(sh.full):
            t_out[pl.ds(at_t + h, 1), :] = jnp.sum(sums[rel, h], axis=0, keepdims=True)
        last = jnp.zeros((1, LANES), F32)
        if sh.spot:
            row = jnp.broadcast_to(jnp.sum(rests[rel], axis=0, keepdims=True), (8, LANES))
            folded = row
            for i in range(1, min(sh.beside, sh.modes)):
                folded = folded + pltpu.roll(row, LANES - i * sh.spot, 1)
            last = folded[:1]
        t_out[pl.ds(at_t + sh.full, 1), :] = last


def ops_copies(ops_hbm, ops_vmem, sems, sh):
    span = sh.group * sh.rows
    return [
        pltpu.make_async_copy(
            ops_hbm.at[pl.ds(i * span, span)], ops_vmem.at[pl.ds(i * span, span)], sems.at[i]
        )
        for i in range(sh.subs // sh.group)
    ]


def product(lowered, ops_vmem, sh, copies=None):
    row = lax.broadcasted_iota(jnp.int32, (sh.pad, sh.rows), 0)
    acc = jnp.zeros((sh.pad, sh.rows), F32)
    span = sh.group * sh.rows
    for i in range(sh.subs // sh.group):
        if copies is not None:
            copies[i].wait()
        part = lax.dot_general(
            lowered,
            ops_vmem[i * span : (i + 1) * span],
            (((1,), (1,)), ((), ())),
            preferred_element_type=F32,
        )
        for j in range(sh.group):
            acc = jnp.where(
                row == i * sh.group + j, part[:, j * sh.rows : (j + 1) * sh.rows], acc
            )
    return rows_of(acc, sh)


def sum_parcels(t_in_ref, sh):
    acc = t_in_ref[0]
    for i in range(1, sh.ndev):
        acc = acc + t_in_ref[i]
    return acc


def pick(t_sum, sh, index):
    return total(jnp.where(sh.scalar_at(index), t_sum, 0.0))


def norm2(t_vec, sh):
    return total(jnp.where(sh.t_mask(), t_vec * t_vec, 0.0))


def send_t(t_scr, scalars, sh, t_out):
    payload = jnp.where(sh.t_mask(), t_scr[...], 0.0)
    for index, value in scalars.items():
        payload = jnp.where(sh.scalar_at(index), value, payload)
    if len(t_out.shape) == 2:
        t_out[...] = payload
    else:
        for i in range(sh.ndev):
            t_out[i] = payload


def pack_kernel(
    sh, place_ref, count_ref, traces_hbm, rhs_hbm, send_hbm, load_hbm, factor_hbm,
    fields_out, parcel_a, parcel_b, factor_out, t_out,
    slot_scr, traces_ref, rhs_ref, send_ref, load_ref, factor_ref, sems,
):
    copies = [
        pltpu.make_async_copy(source, target, sems.at[i])
        for i, (source, target) in enumerate(
            (
                (factor_hbm, factor_ref),
                (load_hbm, load_ref),
                (send_hbm, send_ref),
                (rhs_hbm, rhs_ref),
                (traces_hbm, traces_ref),
            )
        )
    ]
    for copy in copies:
        copy.start()
    for copy in copies:
        copy.wait()
    me, odd = place_ref[0], place_ref[1]
    group = -(-(sh.modes + 1) // 8) * 8
    filler = jnp.zeros((group - sh.modes - 1, sh.order), F32)
    row = lax.broadcasted_iota(jnp.int32, (group, sh.order), 0)
    tiles = []
    for s in range(sh.subs):
        tile = jnp.concatenate([traces_ref[s], rhs_ref[s : s + 1, :], filler], axis=0)
        tiles.append(jnp.where((row < count_ref[s]) | (row >= sh.modes), tile, 0.0))
    by_sub = jnp.concatenate(tiles, axis=0)
    shape = ((sh.modes + 1) * sh.pad, sh.subs * group)
    out_row = lax.broadcasted_iota(jnp.int32, shape, 0)
    mode = floor_div(out_row, sh.pad, sh.modes + 1)
    sub = out_row - mode * sh.pad
    hit = lax.broadcasted_iota(jnp.int32, shape, 1) == sub * group + mode
    order = jnp.where(hit & (sub < sh.subs), 1.0, 0.0).astype(BF16)
    by_mode = select_dot(order, by_sub)
    fields = []
    for k in range(sh.modes + 1):
        fields.append(rows_of(by_mode[k * sh.pad : (k + 1) * sh.pad], sh))
        fields_out[k] = fields[k]
    fields = jnp.concatenate(fields, axis=1)

    shape = (sh.tile_rows, sh.subs * sh.modes)
    out_row = lax.broadcasted_iota(jnp.int32, shape, 0)
    mode = floor_div(out_row, sh.pad, sh.modes)
    sub = out_row - mode * sh.pad
    hit = lax.broadcasted_iota(jnp.int32, shape, 1) == sub * sh.modes + mode
    order = jnp.where(hit & (sub < sh.subs), 1.0, 0.0).astype(BF16)
    factor = select_dot(order, factor_ref[...])
    factor = jnp.concatenate(
        [factor, jnp.zeros((sh.tile_rows, sh.wide - sh.cols), F32)], axis=1
    )
    tiles = [factor[:, h * LANES : (h + 1) * LANES] for h in range(sh.full)]
    rest = factor[:, sh.full * LANES :]
    for tile in range(sh.rest_tiles):
        side = jnp.zeros((sh.pad, LANES), F32)
        for i in range(min(sh.beside, sh.modes - tile * sh.beside)):
            mode = tile * sh.beside + i
            part = rest[mode * sh.pad : (mode + 1) * sh.pad]
            side = side + (pltpu.roll(part, i * sh.spot, 1) if i else part)
        tiles.append(side)
    factor = jnp.concatenate(tiles, axis=0)
    factor_out[...] = factor

    width = sh.slot_lanes
    lists = send_ref[...].astype(F32)
    lists = jnp.concatenate([lists, jnp.full((2, width - sh.slots), -1.0, F32)], axis=1)
    lists = jnp.concatenate([lists, jnp.full((6, width), -1.0, F32)], axis=0).astype(jnp.int32)
    sub = floor_div(lists, sh.blocks, sh.subs)
    lists = jnp.where(lists >= 0, (lists - sub * sh.blocks) * sh.pad + sub, -1).astype(F32)
    turned = jnp.transpose(lists)
    at = pl.multiple_of((me % 2) * sh.half_slots, 8)
    for out, row in ((parcel_a, 1 - odd), (parcel_b, odd)):
        names = jnp.where(row == 0, lists[0:1], lists[1:2])
        column = jnp.where(row == 0, turned[:, 0:1], turned[:, 1:2])
        slot_scr[...] = jnp.broadcast_to(column, (width, LANES))
        line = slot_scr[pl.ds(at, sh.half_slots), :].astype(jnp.int32)
        picked = select_dot(repeated_one_hot(line, sh.all_rows), fields)
        for k in range(sh.planes):
            out[k * sh.half_slots : (k + 1) * sh.half_slots, :] = picked[
                :, k * LANES : (k + 1) * LANES
            ]
        for i in range(width // LANES):
            out[sh.names_at + 8 * i : sh.names_at + 8 * (i + 1), :] = jnp.broadcast_to(
                names[:, i * LANES : (i + 1) * LANES], (8, LANES)
            )
        out[sh.parcel :, :] = factor

    lane = lax.broadcasted_iota(jnp.int32, (8, sh.subs * sh.modes), 1)
    kept = lane < 0
    for s in range(sh.subs):
        kept = kept | ((lane >= s * sh.modes) & (lane < s * sh.modes + count_ref[s]))
    load = jnp.where(kept, jnp.broadcast_to(load_ref[...], kept.shape), 0.0)
    part = jnp.dot(
        load, factor_ref[...], preferred_element_type=F32, precision=lax.Precision.HIGHEST
    )
    part = jnp.concatenate([part, jnp.zeros((8, sh.wide - sh.cols), F32)], axis=1)[:1]
    payload = rows_of_lanes(part)
    for i in range(sh.ndev):
        t_out[i] = payload


def setup_kernel(
    sh, place_ref, partner_ref, fields_ref, near_a, near_b, core_ref,
    tr_out, pt_out, jump_out, ep_out, ept_out, sub_scr,
):
    me, odd = place_ref[0], place_ref[1]
    codes = partner_ref[...]
    codes = jnp.concatenate(
        [codes, jnp.full((sh.pad - sh.subs, sh.blocks), -1, jnp.int32)], axis=0
    )
    code = jnp.concatenate(
        [jnp.broadcast_to(codes[:, b : b + 1], (sh.pad, LANES)) for b in range(sh.blocks)], axis=0
    )
    local_blocks = sh.subs * sh.blocks
    linked = code >= 0
    is_own = linked & (code < local_blocks)
    before = (code >= local_blocks) & (code < local_blocks + sh.slots)
    after = code >= local_blocks + sh.slots
    is_a = (before & (odd == 1)) | (after & (odd == 0))
    slot = jnp.where(before, code - local_blocks, code - local_blocks - sh.slots)
    upper = (slot >= sh.half_slots).astype(jnp.int32)
    other = jnp.where(upper == me % 2, 0, 1)
    own_sub = floor_div(code, sh.blocks, sh.subs)
    line = (code - own_sub * sh.blocks) * sh.pad + own_sub
    source = jnp.where(
        is_own,
        line,
        sh.all_rows
        + other * 2 * sh.half_slots
        + jnp.where(is_a, 0, sh.half_slots)
        + (slot - upper * sh.half_slots),
    )
    source = jnp.where(linked, source, -1)
    chooser = repeated_one_hot(source, sh.all_rows + 4 * sh.half_slots)
    columns = []
    for k in range(sh.planes):
        rows = slice(k * sh.half_slots, (k + 1) * sh.half_slots)
        rows_b = slice(sh.names_at + k * sh.half_slots, sh.names_at + (k + 1) * sh.half_slots)
        columns.append(
            jnp.concatenate(
                [
                    fields_ref[k], near_a[rows, :], near_b[rows, :],
                    core_ref[rows, :], core_ref[rows_b, :],
                ],
                axis=0,
            )
        )
    far = select_dot(chooser, jnp.concatenate(columns, axis=1))
    live = linked.astype(F32)
    for k in range(sh.modes + 1):
        far_k = far[:, k * LANES : (k + 1) * LANES]
        if k < sh.modes:
            tr_out[k] = fields_ref[k] * live
            pt_out[k] = far_k
        else:
            tr_out[k] = fields_ref[k]
            pt_out[k] = fields_ref[k] * live - far_k

    names = []
    for ref in (near_a, near_b):
        parts = []
        for i in range(sh.slot_lanes // LANES):
            tile = ref[sh.names_at + 8 * i : sh.names_at + 8 * (i + 1), :]
            parts.append(jnp.broadcast_to(jnp.transpose(tile)[:, 0:1], (LANES, LANES)))
        names.append(jnp.concatenate(parts, axis=0))
    named = select_dot(
        repeated_one_hot(slot, sh.slot_lanes), jnp.concatenate(names, axis=1)
    ).astype(jnp.int32)
    far_line = jnp.where(is_own, line, jnp.where(is_a, named[:, :LANES], named[:, LANES:]))
    wide = (sh.all_rows, LANES)
    own_line = lax.broadcasted_iota(jnp.int32, wide, 0)

    def piece_row(block, sub, where):
        member = floor_div(block, sh.piece_blocks, sh.crs)
        place = sh.slot_of(jnp.bitwise_xor(member, me)) * 3 + where
        return place * sh.piece + (block - member * sh.piece_blocks) * sh.pad + sub

    def split(value):
        block = floor_div(value, sh.pad, sh.blocks)
        return block, value - block * sh.pad

    far_block, far_sub = split(far_line)
    own_block, own_sub = split(own_line)
    where = jnp.where(is_own, 0, jnp.where(is_a, 1, 2))
    own_col = jnp.where(linked, piece_row(own_block, own_sub, 0), -1)
    far_col = jnp.where(linked, piece_row(far_block, far_sub, where), -1)
    columns = 3 * sh.crs * sh.piece
    jump_out[...] = repeated_one_hot(own_col, columns) - repeated_one_hot(far_col, columns)
    far_sub = jnp.where(linked, where * sh.pad + far_sub, -1)
    pick_far = repeated_one_hot(far_sub, 3 * sh.pad)
    ep_out[...] = pick_far
    sub_scr[...] = far_sub.astype(F32)
    mine = sub_scr[pl.ds(pl.multiple_of(me * sh.piece, 16), sh.piece), :]
    mine = jnp.transpose(mine)[: 3 * sh.pad] if 3 * sh.pad <= LANES else jnp.transpose(mine)
    row = lax.broadcasted_iota(jnp.int32, (3 * sh.pad, sh.piece), 0).astype(F32)
    ept_out[...] = jnp.where(mine[:1] == row, 1.0, 0.0).astype(BF16)


def first_kernel(
    sh, place_ref, tr_ref, pt_ref, ep_ref, ept_ref, t_in, w0, w1, ops_hbm,
    lam_out, q_out, t_out, t_scr, ops_vmem, sems,
):
    copies = ops_copies(ops_hbm, ops_vmem, sems, sh)
    for copy in copies:
        copy.start()
    me = place_ref[0]
    w_refs = (w0, w1)
    for j in range(sh.crs):
        acc = t_in[j]
        for i in range(j + sh.crs, sh.ndev, sh.crs):
            acc = acc + t_in[i]
        t_scr[j * sh.halves : (j + 1) * sh.halves, :] = acc
    lam = lift(tr_ref, pt_ref, ep_ref, w_refs, t_scr, me, sh)
    lam_out[...] = lam
    q = product(lanes_of(2.0 * lam, sh).astype(BF16), ops_vmem, sh, copies)
    q_out[...] = q
    at = pl.multiple_of(me * sh.piece, 16)
    value = tr_ref[sh.modes, pl.ds(at, sh.piece), :] - 2.0 * q
    coarse_part(value, tr_ref, pt_ref, ept_ref, w_refs, me, sh, t_scr)
    send_t(t_scr, {}, sh, t_out)


def second_kernel(
    sh, place_ref, tr_ref, pt_ref, jump_ref, ep_ref, ept_ref, q0, q1, t_in, w0, w1, ops_hbm,
    state_ref, tr0_out, q_out, t_out, ops_out, t_scr, sems,
):
    copies = ops_copies(ops_hbm, ops_out, sems, sh)
    for copy in copies:
        copy.start()
    me = place_ref[0]
    w_refs = (w0, w1)
    applied = select_dot(jump_ref[...], jnp.concatenate([q0[...], q1[...]], axis=0))
    tr0_out[...] = sum_parcels(t_in, sh)
    back = lift(tr_ref, pt_ref, ep_ref, w_refs, tr0_out, me, sh)
    residual = tr_ref[sh.modes] - applied
    jump_r = pt_ref[sh.modes] - 2.0 * applied
    jump_d = jump_r - 2.0 * back
    state_ref[0] = residual
    state_ref[1] = jump_r
    state_ref[2] = residual - back
    state_ref[3] = jump_d
    q = product(lanes_of(jump_d, sh).astype(BF16), ops_out, sh, copies)
    q_out[...] = q
    coarse_part(2.0 * q, tr_ref, pt_ref, ept_ref, w_refs, me, sh, t_scr)
    mine = pl.ds(pl.multiple_of(me * sh.piece, 16), sh.piece)
    own_r = state_ref[0, mine, :]
    send_t(
        t_scr,
        {
            0: total(state_ref[3, mine, :] * q),
            1: total(state_ref[1, mine, :] * q),
            2: total(own_r * own_r),
        },
        sh,
        t_out,
    )


def square_kernel(sh, place_ref, jump_ref, q0, q1, t_in, applied_out, t_out):
    me = place_ref[0]
    applied_out[...] = select_dot(jump_ref[...], jnp.concatenate([q0[...], q1[...]], axis=0))
    at = pl.multiple_of(me * sh.piece, 16)
    mine = applied_out[pl.ds(at, sh.piece), :]
    payload = jnp.where(sh.scalar_at(3), total(mine * mine), t_in[...])
    for i in range(sh.ndev):
        t_out[i] = payload


def third_kernel(
    sh, place_ref, tr_ref, pt_ref, ep_ref, ept_ref, applied_ref, t_in, w0, w1, tr0_ref,
    state_ref, lam_ref, ops_ref,
    next_out, tr1_out, q_out, t_out, t_scr, jd_scr,
):
    me = place_ref[0]
    w_refs = (w0, w1)
    sums = sum_parcels(t_in, sh)
    tr0 = tr0_ref[...]
    d_a, r_a, r_r, a_a = (pick(sums, sh, i) for i in range(4))
    rw0 = r_r - norm2(tr0, sh)
    alpha = rw0 / d_a
    tr1 = tr0 - alpha * sums
    rw1 = (r_r - 2.0 * alpha * r_a + alpha * alpha * a_a) - norm2(tr1, sh)
    beta = rw1 / rw0
    tr1_out[...] = jnp.where(sh.scalar_at(0), rw1, tr1)
    back = lift(tr_ref, pt_ref, ep_ref, w_refs, tr1_out, me, sh)
    applied = applied_ref[...]
    direction = state_ref[2]
    jump_d = (state_ref[1] - 2.0 * alpha * applied - 2.0 * back) + beta * state_ref[3]
    jd_scr[...] = jump_d
    residual = state_ref[0] - alpha * applied
    next_out[0] = residual
    next_out[1] = (residual - back) + beta * direction
    next_out[2] = lam_ref[...] + alpha * direction
    q = product(lanes_of(jump_d, sh).astype(BF16), ops_ref, sh)
    q_out[...] = q
    coarse_part(2.0 * q, tr_ref, pt_ref, ept_ref, w_refs, me, sh, t_scr)
    at = pl.multiple_of(me * sh.piece, 16)
    send_t(t_scr, {0: total(jd_scr[pl.ds(at, sh.piece), :] * q)}, sh, t_out)


def last_kernel(
    sh, place_ref, tr_ref, pt_ref, jump_ref, ep_ref, q0, q1, t_in, w0, w1, tr1_ref, state_ref,
    lam_out, p_out, t_scr,
):
    me = place_ref[0]
    sums = sum_parcels(t_in, sh)
    tr1 = tr1_ref[...]
    alpha = pick(tr1, sh, 0) / pick(sums, sh, 0)
    t_scr[...] = tr1 - alpha * sums
    applied = select_dot(jump_ref[...], jnp.concatenate([q0[...], q1[...]], axis=0))
    back = lift(tr_ref, pt_ref, ep_ref, (w0, w1), t_scr, me, sh)
    lam = state_ref[2] + alpha * state_ref[1]
    projected = (state_ref[0] - alpha * applied) - back
    lam_out[...] = lanes_of(lam, sh)[: sh.subs]
    p_out[...] = lanes_of(projected, sh)[: sh.subs]


def permute(value, move):
    sub_num, crs_num = lax.axis_size("sub"), lax.axis_size("crs")
    pairs = []
    for i in range(sub_num):
        for j in range(crs_num):
            to_i, to_j = move(i, j)
            if 0 <= to_i < sub_num:
                pairs.append((i * crs_num + j, to_i * crs_num + to_j))
    return lax.ppermute(value, AXES, pairs)


def swap_a(value):
    return permute(value, lambda i, j: (i ^ 1, j))


def swap_b(value):
    return permute(value, lambda i, j: (((i + 1) ^ 1) - 1, j))


def core_swap(value):
    return permute(value, lambda i, j: (i, j ^ 1))


def x_swaps(value):
    return [
        permute(value, lambda i, j: (i, j ^ (2 * shift)))
        for shift in range(1, lax.axis_size("crs") // 2)
    ]


def spread_pieces(value):
    near = jnp.concatenate([value, swap_a(value), swap_b(value)], axis=0)
    first = jnp.concatenate([near] + x_swaps(near), axis=0)
    return first, core_swap(first)


def local(
    dual_ops, rigid_traces, coarse_factor, partner, send_list, mode_count, dual_rhs, rigid_load
):
    sh = Shape(dual_ops, rigid_traces, coarse_factor, partner, send_list)
    modes, subs = sh.modes, sh.subs
    place = jnp.stack([lax.axis_index("crs"), lax.axis_index("sub") % 2]).astype(jnp.int32)

    vmem = pl.BlockSpec(memory_space=pltpu.VMEM)
    smem = pl.BlockSpec(memory_space=pltpu.SMEM)
    hbm = pl.BlockSpec(memory_space=pltpu.HBM)

    tags = {"v": vmem, "k": vmem, "s": smem, "h": hbm}

    def call(kernel, ins, outs, scratch, *operands, name, cost):
        operands = [
            pltpu.with_memory_space_constraint(x, pltpu.HBM) if tag == "h" else x
            for tag, x in zip(ins, operands)
        ]
        return pl.pallas_call(
            functools.partial(kernel, sh),
            out_shape=[
                pltpu.VMEM(s, t) if tag == "k" else jax.ShapeDtypeStruct(s, t)
                for tag, s, t in outs
            ],
            in_specs=[smem] + [tags[tag] for tag in ins],
            out_specs=[tags[tag] for tag, _, _ in outs],
            scratch_shapes=scratch,
            compiler_params=pltpu.CompilerParams(vmem_limit_bytes=24 * 1024 * 1024),
            cost_estimate=pl.CostEstimate(flops=0, bytes_accessed=cost, transcendentals=0),
            name=name,
        )(place, *operands)

    rows = (sh.all_rows, LANES)
    t_shape = ("v", (sh.t_rows, LANES), F32)
    parcels = ("v", (sh.ndev, sh.t_rows, LANES), F32)
    columns = ("v", (sh.ndev, sh.halves, LANES), F32)
    q_shape = ("v", (sh.piece, LANES), F32)
    field_shape = ("v", (modes + 1,) + rows, F32)
    t_scratch = pltpu.VMEM((sh.t_rows, LANES), F32)
    ops = dual_ops.reshape(subs * sh.rows, sh.order)
    ops_kept = ("k", ops.shape, BF16)
    ops_sems = subs // sh.group
    long = dual_ops.size * 2

    def exchange(parcel):
        return lax.all_to_all(parcel, AXES, 0, 0)

    def stack(count):
        return (count,) + rows

    parcel_shape = ("v", (sh.parcel + sh.factor_rows, LANES), F32)
    raw = (rigid_traces, dual_rhs, send_list, rigid_load[None, :], coarse_factor)
    fields, parcel_a, parcel_b, factor, t_part = call(
        pack_kernel, "shhhhh",
        [field_shape, parcel_shape, parcel_shape, ("v", (sh.factor_rows, LANES), F32), columns],
        [pltpu.VMEM((sh.slot_lanes, LANES), F32)]
        + [pltpu.VMEM(x.shape, x.dtype) for x in raw]
        + [pltpu.SemaphoreType.DMA((len(raw),))],
        mode_count, *raw, name="pack", cost=8_000_000,
    )
    near_a, near_b = swap_a(parcel_a), swap_b(parcel_b)
    factor_x = x_swaps(factor)
    t_part, near_b = lax.optimization_barrier((t_part, near_b))
    t_in = exchange(t_part)
    halves = core_swap(jnp.concatenate([near_a[: sh.names_at], near_b[: sh.names_at]], axis=0))
    factor_ab = jnp.concatenate([near_a[sh.parcel :], near_b[sh.parcel :]], axis=0)
    w0 = [factor, factor_ab]
    for own, pair in zip(factor_x, x_swaps(factor_ab)):
        w0 += [own, pair]
    traces, far_traces, jumper, far_pick, far_put = call(
        setup_kernel, "vvvvv",
        [
            field_shape, field_shape,
            ("v", (sh.all_rows, 3 * sh.crs * sh.piece), BF16),
            ("v", (sh.all_rows, 3 * sh.pad), BF16),
            ("v", (3 * sh.pad, sh.piece), BF16),
        ],
        [pltpu.VMEM(rows, F32)],
        partner, fields, near_a, near_b, halves, name="setup", cost=6_000_000,
    )
    rider = jnp.concatenate([t_in[0, :1], far_traces[0, :7]], axis=0)
    w0 = jnp.concatenate(w0 + [rider], axis=0)
    w1 = core_swap(w0)
    lam0, q, t_part = call(
        first_kernel, "vvvvvvvh",
        [("v", rows, F32), q_shape, parcels],
        [t_scratch, pltpu.VMEM(ops.shape, BF16), pltpu.SemaphoreType.DMA((ops_sems,))],
        traces, far_traces, far_pick, far_put, t_in, w0, w1, ops, name="first", cost=long,
    )
    q0, q1 = spread_pieces(q)
    t_in = exchange(t_part)

    state0, tr0, q, t_part, ops_vmem = call(
        second_kernel, "vvvvvvvvvvh",
        [("v", stack(4), F32), t_shape, q_shape, t_shape, ops_kept],
        [t_scratch, pltpu.SemaphoreType.DMA((ops_sems,))],
        traces, far_traces, jumper, far_pick, far_put, q0, q1, t_in, w0, w1, ops,
        name="second", cost=long,
    )
    q0, q1 = spread_pieces(q)
    applied, t_part = call(
        square_kernel, "vvvv", [("v", rows, F32), parcels], [],
        jumper, q0, q1, t_part, name="square", cost=2_000_000,
    )
    t_in = exchange(t_part)

    state1, tr1, q, t_part = call(
        third_kernel, "vvvvvvvvvvvv",
        [("v", stack(3), F32), t_shape, q_shape, parcels],
        [t_scratch, pltpu.VMEM(rows, F32)],
        traces, far_traces, far_pick, far_put, applied, t_in, w0, w1, tr0, state0, lam0, ops_vmem,
        name="third", cost=long,
    )
    q0, q1 = spread_pieces(q)
    t_in = exchange(t_part)

    return tuple(
        call(
            last_kernel, "vvvvvvvvvvv",
            [("v", (subs, sh.order), F32)] * 2,
            [t_scratch],
            traces, far_traces, jumper, far_pick, q0, q1, t_in, w0, w1, tr1, state1,
            name="last", cost=4_000_000,
        )
    )


def body(*args):
    dual_ops, _, _, partner = args[:4]
    crs_num, sub_num = lax.axis_size("crs"), lax.axis_size("sub")
    whole_blocks = (
        dual_ops.shape[2] // partner.shape[1] == LANES and dual_ops.shape[1] % LANES == 0
    )
    fits = whole_blocks and args[2].shape[1] % LANES + 8 <= LANES
    if fits and crs_num % 2 == 0 and crs_num & (crs_num - 1) == 0 and sub_num % 2 == 0:
        return local(*args)
    return plain(*args)


def solution(mesh):
    return jax.shard_map(
        body,
        mesh=mesh,
        in_specs=(
            P("sub", "crs", None),
            P("sub", None, None),
            P("sub", "crs"),
            P("sub", None),
            P("sub", None),
            P("sub"),
            P("sub", None),
            P("sub"),
        ),
        out_specs=(P("sub", None), P("sub", None)),
        check_vma=False,
    )
```

```python
import functools

import jax
import jax.numpy as jnp
from jax import lax
from jax.experimental import pallas as pl
from jax.experimental.pallas import tpu as pltpu
from jax.sharding import PartitionSpec as P

ITERATIONS = 2
AXES = ("sub", "crs")
LANES = 128
F32 = jnp.float32
BF16 = jnp.bfloat16


def with_halo(block, sides, width):
    for axis, dim in sides:
        count = lax.axis_size(axis)
        forward = [(i, i + 1) for i in range(count - 1)]
        backward = [(target, source) for source, target in forward]
        low = lax.ppermute(
            lax.slice_in_dim(block, block.shape[dim] - width, None, axis=dim), axis, forward
        )
        high = lax.ppermute(lax.slice_in_dim(block, 0, width, axis=dim), axis, backward)
        block = jnp.concatenate([low, block, high], axis=dim)
    return block


def plain(
    dual_ops, rigid_traces, coarse_factor, partner, send_list, mode_count, dual_rhs, rigid_load
):
    sub_count = dual_ops.shape[0]
    block_num = partner.shape[1]
    order_len = dual_ops.shape[2]
    block_len = order_len // block_num
    local_blocks = sub_count * block_num
    mode_num = rigid_traces.shape[1]
    links = partner.reshape(local_blocks)
    linked = (links >= 0)[:, None]
    source = jnp.maximum(links, 0)
    sending = (send_list >= 0)[:, :, None]
    picked = jnp.maximum(send_list, 0)
    mode_mask = (jnp.arange(mode_num, dtype=jnp.int32)[None, :] < mode_count[:, None]).astype(F32)

    def jump(vector):
        pieces = vector.reshape(local_blocks, block_len)
        parcels = jnp.where(sending, pieces[picked], 0.0)
        arrived = with_halo(parcels, (("sub", 0),), 1)
        incoming = jnp.concatenate([arrived[0], arrived[3]], axis=0)
        gathered = jnp.concatenate([pieces, incoming], axis=0)
        return jnp.where(linked, pieces - gathered[source], 0.0).reshape(vector.shape)

    def operator(vector):
        lowered = jump(vector).astype(BF16)
        partial_rows = jnp.einsum("srk,sk->sr", dual_ops, lowered, preferred_element_type=F32)
        full_rows = lax.all_gather(partial_rows, "crs", axis=1, tiled=True)
        return jump(full_rows)

    def restrict(vector):
        traced = jnp.einsum(
            "skm,sm->sk", rigid_traces, jump(vector), precision=lax.Precision.HIGHEST
        )
        return (traced * mode_mask).reshape(sub_count * mode_num)

    def expand(coarse_vec):
        scaled = coarse_vec.reshape(sub_count, mode_num) * mode_mask
        spread = jnp.einsum("skm,sk->sm", rigid_traces, scaled, precision=lax.Precision.HIGHEST)
        return jump(spread)

    def coarse(restricted, squares):
        column_part = jnp.dot(restricted, coarse_factor, precision=lax.Precision.HIGHEST)
        column_sum, total_sq = lax.psum((column_part, squares), "sub")
        back_part = jnp.dot(coarse_factor, column_sum, precision=lax.Precision.HIGHEST)
        solved, folded = lax.psum((back_part, jnp.sum(column_sum * column_sum)), "crs")
        return (solved, total_sq, folded)

    def project(residual):
        solved, total_sq, folded = coarse(restrict(residual), jnp.sum(residual * residual))
        return (residual - expand(solved), total_sq - folded)

    start_load = rigid_load * mode_mask.reshape(sub_count * mode_num)
    start_solved, _, _ = coarse(start_load, jnp.zeros((), F32))
    multipliers = expand(start_solved)
    residual = dual_rhs - operator(multipliers)
    projected, inner_rw = project(residual)
    direction = projected
    for _ in range(ITERATIONS):
        applied = operator(direction)
        curvature = lax.psum(jnp.sum(direction * applied), "sub")
        step_len = inner_rw / curvature
        multipliers = multipliers + step_len * direction
        residual = residual - step_len * applied
        projected, next_rw = project(residual)
        direction = projected + next_rw / inner_rw * direction
        inner_rw = next_rw
    return (multipliers, projected)


def split3(value):
    high = value.astype(BF16)
    rest = value - high.astype(F32)
    mid = rest.astype(BF16)
    low = (rest - mid.astype(F32)).astype(BF16)
    return high, mid, low


def select_dot(chooser, value):
    width = value.shape[1]
    wide = jnp.dot(
        chooser, jnp.concatenate(split3(value), axis=1), preferred_element_type=F32
    )
    return (wide[:, 2 * width :] + wide[:, width : 2 * width]) + wide[:, :width]


def one_hot(column, width):
    rows = column.shape[0]
    return (lax.broadcasted_iota(jnp.int32, (rows, width), 1) == column).astype(F32)


def repeated_one_hot(code, width):
    lane = lax.broadcasted_iota(jnp.int32, code.shape, 1)
    tiles = [(lane + at == code).astype(F32) for at in range(0, width, LANES)]
    return jnp.concatenate(tiles, axis=1)[:, :width].astype(BF16)


def floor_div(value, by, most):
    out = jnp.zeros(value.shape, jnp.int32)
    for i in range(1, most):
        out = out + (value >= i * by).astype(jnp.int32)
    return out


def total(value):
    return jnp.sum(jnp.sum(value, axis=0, keepdims=True), axis=1, keepdims=True)


class Shape:
    def __init__(self, dual_ops, rigid_traces, coarse_factor, partner, send_list):
        self.subs, self.rows, self.order = dual_ops.shape
        self.blocks = partner.shape[1]
        self.modes = rigid_traces.shape[1]
        self.slots = send_list.shape[1]
        self.crs = lax.axis_size("crs")
        self.ndev = lax.axis_size("sub") * self.crs
        self.pad = -(-self.subs // 16) * 16
        self.all_rows = self.blocks * self.pad
        self.piece_blocks = self.rows // LANES
        self.piece = self.piece_blocks * self.pad
        self.half_slots = -(-self.slots // 16) * 8
        self.planes = self.modes + 1
        self.group = 2 if self.subs % 2 == 0 else 1
        self.names_at = self.planes * self.half_slots
        self.slot_lanes = -(-2 * self.half_slots // LANES) * LANES
        self.parcel = self.names_at + 8 * (self.slot_lanes // LANES)
        self.cols = coarse_factor.shape[1]
        self.full = self.cols // LANES
        self.spot = self.cols % LANES
        self.halves = self.full + 1
        self.wide = self.halves * LANES
        self.t_rows = self.crs * self.halves
        self.sum_rows = -(-self.halves // 8) * 8
        self.tile_rows = self.modes * self.pad
        self.beside = LANES // max(self.spot, 1)
        self.rest_tiles = -(-self.modes // self.beside) if self.spot else 0
        self.factor_rows = self.full * self.tile_rows + self.rest_tiles * self.pad

    def scalar_at(self, index):
        rows = lax.broadcasted_iota(jnp.int32, (self.t_rows, LANES), 0)
        lanes = lax.broadcasted_iota(jnp.int32, (self.t_rows, LANES), 1)
        return (rows == self.halves - 1) & (lanes == self.spot + index)

    def t_mask(self):
        rows = lax.broadcasted_iota(jnp.int32, (self.t_rows, LANES), 0)
        lanes = lax.broadcasted_iota(jnp.int32, (self.t_rows, LANES), 1)
        return (rows % self.halves < self.halves - 1) | (lanes < self.spot)

    def slot_of(self, rel):
        return (rel % 2) * (self.crs // 2) + rel // 2


def rows_of(value, sh):
    return jnp.concatenate(
        [value[:, b * LANES : (b + 1) * LANES] for b in range(value.shape[1] // LANES)], axis=0
    )


def rows_of_lanes(value):
    return jnp.concatenate(
        [value[:, at : at + LANES] for at in range(0, value.shape[1], LANES)], axis=0
    )


def lanes_of(value, sh):
    return jnp.concatenate(
        [value[b * sh.pad : (b + 1) * sh.pad] for b in range(value.shape[0] // sh.pad)], axis=1
    )


def factor_tile(w_refs, sh, rel, where, at):
    slot = sh.slot_of(rel)
    xs = sh.crs // 2
    base = ((slot % xs) * 3 + where) * sh.factor_rows + at
    return w_refs[slot // xs][base : base + sh.pad, :]


def full_tile(w_refs, sh, rel, where, mode, h):
    return factor_tile(w_refs, sh, rel, where, h * sh.tile_rows + mode * sh.pad)


def rest_tile(w_refs, sh, rel, where, tile):
    return factor_tile(w_refs, sh, rel, where, sh.full * sh.tile_rows + tile * sh.pad)


def lane_group(sh, shape):
    lane = lax.broadcasted_iota(jnp.int32, shape, 1)
    return floor_div(lane, sh.spot, sh.beside + 1)


def coarse_back(w_refs, t_ref, me, sh):
    t_row, t_rest = {}, []
    lane = lax.broadcasted_iota(jnp.int32, (8, LANES), 1)
    for rel in range(sh.crs):
        at = jnp.bitwise_xor(me, rel) * sh.halves
        for h in range(sh.full):
            t_row[rel, h] = t_ref[pl.ds(at + h, 1), :]
        if sh.spot:
            rest = jnp.broadcast_to(t_ref[pl.ds(at + sh.full, 1), :], (8, LANES))
            rest = jnp.where(lane < sh.spot, rest, 0.0)
            spread = rest
            for i in range(1, sh.beside):
                spread = spread + pltpu.roll(rest, i * sh.spot, 1)
            t_rest.append(spread[:1])
    rests = {}
    for where in range(3):
        for tile in range(sh.rest_tiles):
            acc = jnp.zeros((sh.pad, LANES), F32)
            for rel in range(sh.crs):
                acc += rest_tile(w_refs, sh, rel, where, tile) * t_rest[rel]
            rests[where, tile] = acc
    group = lane_group(sh, (sh.pad, LANES)) if sh.spot else None
    columns = []
    for mode in range(sh.modes):
        parts = []
        for where in range(3):
            acc = jnp.zeros((sh.pad, LANES), F32)
            if sh.spot:
                mine = group == mode % sh.beside
                acc = jnp.where(mine, rests[where, mode // sh.beside], 0.0)
            for rel in range(sh.crs):
                for h in range(sh.full):
                    acc += full_tile(w_refs, sh, rel, where, mode, h) * t_row[rel, h]
            parts.append(
                jnp.broadcast_to(jnp.sum(acc, axis=1, keepdims=True), (sh.pad, LANES))
            )
        columns.append(jnp.concatenate(parts, axis=0))
    return jnp.concatenate(columns, axis=1)


def lift(tr_ref, pt_ref, ep_ref, w_refs, t_ref, me, sh):
    spread = coarse_back(w_refs, t_ref, me, sh)
    far = select_dot(ep_ref[...], spread)
    out = jnp.zeros((sh.all_rows, LANES), F32)
    for mode in range(sh.modes):
        own = spread[: sh.pad, mode * LANES : (mode + 1) * LANES]
        own = jnp.concatenate([own] * sh.blocks, axis=0)
        out += tr_ref[mode] * own - pt_ref[mode] * far[:, mode * LANES : (mode + 1) * LANES]
    return out


def coarse_part(value, tr_ref, pt_ref, ept_ref, w_refs, me, sh, t_out):
    at = pl.multiple_of(me * sh.piece, 16)
    own, far = [], []
    for mode in range(sh.modes):
        mine = tr_ref[mode, pl.ds(at, sh.piece), :] * value
        acc = mine[: sh.pad]
        for b in range(1, sh.piece_blocks):
            acc = acc + mine[b * sh.pad : (b + 1) * sh.pad]
        own.append(acc)
        far.append(pt_ref[mode, pl.ds(at, sh.piece), :] * value)
    moved = select_dot(ept_ref[...], jnp.concatenate(far, axis=1))
    sums, rests = {}, {}
    group = lane_group(sh, (sh.pad, LANES)) if sh.spot else None
    side = {}

    def add(table, key, term):
        table[key] = table[key] + term if key in table else term

    for mode in range(sh.modes):
        moved_k = moved[:, mode * LANES : (mode + 1) * LANES]
        for where in range(3):
            part = -moved_k[where * sh.pad : (where + 1) * sh.pad]
            if where == 0:
                part = part + own[mode]
            weight = jnp.broadcast_to(jnp.sum(part, axis=1, keepdims=True), (sh.pad, LANES))
            for rel in range(sh.crs):
                for h in range(sh.full):
                    add(sums, (rel, h), full_tile(w_refs, sh, rel, where, mode, h) * weight)
            if sh.spot:
                mine = group == mode % sh.beside
                add(side, (where, mode // sh.beside), jnp.where(mine, weight, 0.0))
    for (where, tile), weight in side.items():
        for rel in range(sh.crs):
            add(rests, rel, rest_tile(w_refs, sh, rel, where, tile) * weight)
    for rel in range(sh.crs):
        at_t = jnp.bitwise_xor(me, rel) * sh.halves
        for h in range(sh.full):
            t_out[pl.ds(at_t + h, 1), :] = jnp.sum(sums[rel, h], axis=0, keepdims=True)
        last = jnp.zeros((1, LANES), F32)
        if sh.spot:
            row = jnp.broadcast_to(jnp.sum(rests[rel], axis=0, keepdims=True), (8, LANES))
            folded = row
            for i in range(1, min(sh.beside, sh.modes)):
                folded = folded + pltpu.roll(row, LANES - i * sh.spot, 1)
            last = folded[:1]
        t_out[pl.ds(at_t + sh.full, 1), :] = last


def ops_copies(ops_hbm, ops_vmem, sems, sh):
    span = sh.group * sh.rows
    return [
        pltpu.make_async_copy(
            ops_hbm.at[pl.ds(i * span, span)], ops_vmem.at[pl.ds(i * span, span)], sems.at[i]
        )
        for i in range(sh.subs // sh.group)
    ]


def product(lowered, ops_vmem, sh, copies=None):
    row = lax.broadcasted_iota(jnp.int32, (sh.pad, sh.rows), 0)
    acc = jnp.zeros((sh.pad, sh.rows), F32)
    wide = lowered.astype(F32)
    for s in range(sh.subs):
        if copies is not None and s % sh.group == 0:
            copies[s // sh.group].wait()
        base = s * sh.rows
        if s % 2 == 0:
            part = lax.dot_general(
                lowered,
                ops_vmem[base : base + sh.rows],
                (((1,), (1,)), ((), ())),
                preferred_element_type=F32,
            )
        else:
            sums = []
            for at in range(base, base + sh.rows, LANES):
                tile = jnp.zeros((LANES, LANES), F32)
                for k in range(0, sh.order, LANES):
                    block = ops_vmem[at : at + LANES, k : k + LANES].astype(F32)
                    tile = tile + block * wide[s : s + 1, k : k + LANES]
                sums.append(jnp.sum(jnp.transpose(tile), axis=0, keepdims=True))
            part = jnp.concatenate(sums, axis=1)
        acc = jnp.where(row == s, part, acc)
    return rows_of(acc, sh)


def sum_parcels(t_in_ref, sh):
    acc = t_in_ref[0]
    for i in range(1, sh.ndev):
        acc = acc + t_in_ref[i]
    return acc


def pick(t_sum, sh, index):
    return total(jnp.where(sh.scalar_at(index), t_sum, 0.0))


def norm2(t_vec, sh):
    return total(jnp.where(sh.t_mask(), t_vec * t_vec, 0.0))


def send_t(t_scr, scalars, sh, t_out):
    payload = jnp.where(sh.t_mask(), t_scr[...], 0.0)
    for index, value in scalars.items():
        payload = jnp.where(sh.scalar_at(index), value, payload)
    if len(t_out.shape) == 2:
        t_out[...] = payload
    else:
        for i in range(sh.ndev):
            t_out[i] = payload


def start_kernel(sh, place_ref, count_ref, load_hbm, factor_hbm, t_out, load_ref, factor_ref, sems):
    copies = [
        pltpu.make_async_copy(load_hbm, load_ref, sems.at[0]),
        pltpu.make_async_copy(factor_hbm, factor_ref, sems.at[1]),
    ]
    for copy in copies:
        copy.start()
    for copy in copies:
        copy.wait()
    lane = lax.broadcasted_iota(jnp.int32, (8, sh.subs * sh.modes), 1)
    kept = lane < 0
    for s in range(sh.subs):
        kept = kept | ((lane >= s * sh.modes) & (lane < s * sh.modes + count_ref[s]))
    load = jnp.where(kept, jnp.broadcast_to(load_ref[...], kept.shape), 0.0)
    part = jnp.dot(
        load, factor_ref[...], preferred_element_type=F32, precision=lax.Precision.HIGHEST
    )
    part = jnp.concatenate([part, jnp.zeros((8, sh.wide - sh.cols), F32)], axis=1)[:1]
    part = rows_of_lanes(part)
    empty = jnp.zeros((sh.sum_rows - sh.halves, LANES), F32)
    t_out[...] = jnp.concatenate([part, empty], axis=0)


def load_kernel(sh, place_ref, ops_hbm, sum_ref, ops_out, sum_out, sems):
    copies = ops_copies(ops_hbm, ops_out, sems, sh)
    for copy in copies:
        copy.start()
    sum_out[...] = sum_ref[...]
    for copy in copies:
        copy.wait()


def pack_kernel(
    sh, place_ref, count_ref, traces_hbm, rhs_hbm, send_hbm, factor_hbm, after_ref,
    fields_out, parcel_a, parcel_b, factor_out,
    slot_scr, traces_ref, rhs_ref, send_ref, factor_ref, sems,
):
    copies = [
        pltpu.make_async_copy(source, target, sems.at[i])
        for i, (source, target) in enumerate(
            (
                (factor_hbm, factor_ref),
                (send_hbm, send_ref),
                (rhs_hbm, rhs_ref),
                (traces_hbm, traces_ref),
            )
        )
    ]
    for copy in copies:
        copy.start()
    for copy in copies:
        copy.wait()
    me, odd = place_ref[0], place_ref[1]
    group = -(-(sh.modes + 1) // 8) * 8
    filler = jnp.zeros((group - sh.modes - 1, sh.order), F32)
    row = lax.broadcasted_iota(jnp.int32, (group, sh.order), 0)
    tiles = []
    for s in range(sh.subs):
        tile = jnp.concatenate([traces_ref[s], rhs_ref[s : s + 1, :], filler], axis=0)
        tiles.append(jnp.where((row < count_ref[s]) | (row >= sh.modes), tile, 0.0))
    by_sub = jnp.concatenate(tiles, axis=0)
    shape = ((sh.modes + 1) * sh.pad, sh.subs * group)
    out_row = lax.broadcasted_iota(jnp.int32, shape, 0)
    mode = floor_div(out_row, sh.pad, sh.modes + 1)
    sub = out_row - mode * sh.pad
    hit = lax.broadcasted_iota(jnp.int32, shape, 1) == sub * group + mode
    order = jnp.where(hit & (sub < sh.subs), 1.0, 0.0).astype(BF16)
    by_mode = select_dot(order, by_sub)
    fields = []
    for k in range(sh.modes + 1):
        fields.append(rows_of(by_mode[k * sh.pad : (k + 1) * sh.pad], sh))
        fields_out[k] = fields[k]
    fields = jnp.concatenate(fields, axis=1)

    shape = (sh.tile_rows, sh.subs * sh.modes)
    out_row = lax.broadcasted_iota(jnp.int32, shape, 0)
    mode = floor_div(out_row, sh.pad, sh.modes)
    sub = out_row - mode * sh.pad
    hit = lax.broadcasted_iota(jnp.int32, shape, 1) == sub * sh.modes + mode
    order = jnp.where(hit & (sub < sh.subs), 1.0, 0.0).astype(BF16)
    factor = select_dot(order, factor_ref[...])
    factor = jnp.concatenate(
        [factor, jnp.zeros((sh.tile_rows, sh.wide - sh.cols), F32)], axis=1
    )
    tiles = [factor[:, h * LANES : (h + 1) * LANES] for h in range(sh.full)]
    rest = factor[:, sh.full * LANES :]
    for tile in range(sh.rest_tiles):
        side = jnp.zeros((sh.pad, LANES), F32)
        for i in range(min(sh.beside, sh.modes - tile * sh.beside)):
            mode = tile * sh.beside + i
            part = rest[mode * sh.pad : (mode + 1) * sh.pad]
            side = side + (pltpu.roll(part, i * sh.spot, 1) if i else part)
        tiles.append(side)
    factor = jnp.concatenate(tiles, axis=0)
    factor_out[...] = factor

    width = sh.slot_lanes
    lists = send_ref[...].astype(F32)
    lists = jnp.concatenate([lists, jnp.full((2, width - sh.slots), -1.0, F32)], axis=1)
    lists = jnp.concatenate([lists, jnp.full((6, width), -1.0, F32)], axis=0).astype(jnp.int32)
    sub = floor_div(lists, sh.blocks, sh.subs)
    lists = jnp.where(lists >= 0, (lists - sub * sh.blocks) * sh.pad + sub, -1).astype(F32)
    turned = jnp.transpose(lists)
    at = pl.multiple_of((me % 2) * sh.half_slots, 8)
    for out, row in ((parcel_a, 1 - odd), (parcel_b, odd)):
        names = jnp.where(row == 0, lists[0:1], lists[1:2])
        column = jnp.where(row == 0, turned[:, 0:1], turned[:, 1:2])
        slot_scr[...] = jnp.broadcast_to(column, (width, LANES))
        line = slot_scr[pl.ds(at, sh.half_slots), :].astype(jnp.int32)
        picked = select_dot(repeated_one_hot(line, sh.all_rows), fields)
        for k in range(sh.planes):
            out[k * sh.half_slots : (k + 1) * sh.half_slots, :] = picked[
                :, k * LANES : (k + 1) * LANES
            ]
        for i in range(width // LANES):
            out[sh.names_at + 8 * i : sh.names_at + 8 * (i + 1), :] = jnp.broadcast_to(
                names[:, i * LANES : (i + 1) * LANES], (8, LANES)
            )
        out[sh.parcel :, :] = factor


def setup_kernel(
    sh, place_ref, partner_ref, fields_ref, near_a, near_b, core_ref,
    tr_out, pt_out, jump_out, ep_out, ept_out, sub_scr,
):
    me, odd = place_ref[0], place_ref[1]
    codes = partner_ref[...]
    codes = jnp.concatenate(
        [codes, jnp.full((sh.pad - sh.subs, sh.blocks), -1, jnp.int32)], axis=0
    )
    code = jnp.concatenate(
        [jnp.broadcast_to(codes[:, b : b + 1], (sh.pad, LANES)) for b in range(sh.blocks)], axis=0
    )
    local_blocks = sh.subs * sh.blocks
    linked = code >= 0
    is_own = linked & (code < local_blocks)
    before = (code >= local_blocks) & (code < local_blocks + sh.slots)
    after = code >= local_blocks + sh.slots
    is_a = (before & (odd == 1)) | (after & (odd == 0))
    slot = jnp.where(before, code - local_blocks, code - local_blocks - sh.slots)
    upper = (slot >= sh.half_slots).astype(jnp.int32)
    other = jnp.where(upper == me % 2, 0, 1)
    own_sub = floor_div(code, sh.blocks, sh.subs)
    line = (code - own_sub * sh.blocks) * sh.pad + own_sub
    source = jnp.where(
        is_own,
        line,
        sh.all_rows
        + other * 2 * sh.half_slots
        + jnp.where(is_a, 0, sh.half_slots)
        + (slot - upper * sh.half_slots),
    )
    source = jnp.where(linked, source, -1)
    chooser = repeated_one_hot(source, sh.all_rows + 4 * sh.half_slots)
    columns = []
    for k in range(sh.planes):
        rows = slice(k * sh.half_slots, (k + 1) * sh.half_slots)
        rows_b = slice(sh.names_at + k * sh.half_slots, sh.names_at + (k + 1) * sh.half_slots)
        columns.append(
            jnp.concatenate(
                [
                    fields_ref[k], near_a[rows, :], near_b[rows, :],
                    core_ref[rows, :], core_ref[rows_b, :],
                ],
                axis=0,
            )
        )
    far = select_dot(chooser, jnp.concatenate(columns, axis=1))
    live = linked.astype(F32)
    for k in range(sh.modes + 1):
        far_k = far[:, k * LANES : (k + 1) * LANES]
        if k < sh.modes:
            tr_out[k] = fields_ref[k] * live
            pt_out[k] = far_k
        else:
            tr_out[k] = fields_ref[k]
            pt_out[k] = fields_ref[k] * live - far_k

    names = []
    for ref in (near_a, near_b):
        parts = []
        for i in range(sh.slot_lanes // LANES):
            tile = ref[sh.names_at + 8 * i : sh.names_at + 8 * (i + 1), :]
            parts.append(jnp.broadcast_to(jnp.transpose(tile)[:, 0:1], (LANES, LANES)))
        names.append(jnp.concatenate(parts, axis=0))
    named = select_dot(
        repeated_one_hot(slot, sh.slot_lanes), jnp.concatenate(names, axis=1)
    ).astype(jnp.int32)
    far_line = jnp.where(is_own, line, jnp.where(is_a, named[:, :LANES], named[:, LANES:]))
    wide = (sh.all_rows, LANES)
    own_line = lax.broadcasted_iota(jnp.int32, wide, 0)

    def piece_row(block, sub, where):
        member = floor_div(block, sh.piece_blocks, sh.crs)
        place = sh.slot_of(jnp.bitwise_xor(member, me)) * 3 + where
        return place * sh.piece + (block - member * sh.piece_blocks) * sh.pad + sub

    def split(value):
        block = floor_div(value, sh.pad, sh.blocks)
        return block, value - block * sh.pad

    far_block, far_sub = split(far_line)
    own_block, own_sub = split(own_line)
    where = jnp.where(is_own, 0, jnp.where(is_a, 1, 2))
    own_col = jnp.where(linked, piece_row(own_block, own_sub, 0), -1)
    far_col = jnp.where(linked, piece_row(far_block, far_sub, where), -1)
    columns = 3 * sh.crs * sh.piece
    jump_out[...] = repeated_one_hot(own_col, columns) - repeated_one_hot(far_col, columns)
    far_sub = jnp.where(linked, where * sh.pad + far_sub, -1)
    pick_far = repeated_one_hot(far_sub, 3 * sh.pad)
    ep_out[...] = pick_far
    sub_scr[...] = far_sub.astype(F32)
    mine = sub_scr[pl.ds(pl.multiple_of(me * sh.piece, 16), sh.piece), :]
    mine = jnp.transpose(mine)[: 3 * sh.pad] if 3 * sh.pad <= LANES else jnp.transpose(mine)
    row = lax.broadcasted_iota(jnp.int32, (3 * sh.pad, sh.piece), 0).astype(F32)
    ept_out[...] = jnp.where(mine[:1] == row, 1.0, 0.0).astype(BF16)


def first_kernel(
    sh, place_ref, tr_ref, pt_ref, ep_ref, ept_ref, w0, w1, ops_ref,
    lam_out, q_out, t_out, t_scr,
):
    me = place_ref[0]
    w_refs = (w0, w1)
    for rel in range(sh.crs):
        at = jnp.bitwise_xor(me, rel) * sh.halves
        base = sh.crs // 2 * 3 * sh.factor_rows + rel // 2 * sh.sum_rows
        for h in range(sh.halves):
            t_scr[pl.ds(at + h, 1), :] = w_refs[rel % 2][base + h : base + h + 1, :]
    lam = lift(tr_ref, pt_ref, ep_ref, w_refs, t_scr, me, sh)
    lam_out[...] = lam
    q = product(lanes_of(2.0 * lam, sh).astype(BF16), ops_ref, sh)
    q_out[...] = q
    at = pl.multiple_of(me * sh.piece, 16)
    value = tr_ref[sh.modes, pl.ds(at, sh.piece), :] - 2.0 * q
    coarse_part(value, tr_ref, pt_ref, ept_ref, w_refs, me, sh, t_scr)
    send_t(t_scr, {}, sh, t_out)


def second_kernel(
    sh, place_ref, tr_ref, pt_ref, jump_ref, ep_ref, ept_ref, q0, q1, t_in, w0, w1, ops_hbm,
    state_ref, tr0_out, q_out, t_out, ops_out, t_scr, sems,
):
    copies = ops_copies(ops_hbm, ops_out, sems, sh)
    for copy in copies:
        copy.start()
    me = place_ref[0]
    w_refs = (w0, w1)
    applied = select_dot(jump_ref[...], jnp.concatenate([q0[...], q1[...]], axis=0))
    tr0_out[...] = sum_parcels(t_in, sh)
    back = lift(tr_ref, pt_ref, ep_ref, w_refs, tr0_out, me, sh)
    residual = tr_ref[sh.modes] - applied
    jump_r = pt_ref[sh.modes] - 2.0 * applied
    jump_d = jump_r - 2.0 * back
    state_ref[0] = residual
    state_ref[1] = jump_r
    state_ref[2] = residual - back
    state_ref[3] = jump_d
    q = product(lanes_of(jump_d, sh).astype(BF16), ops_out, sh, copies)
    q_out[...] = q
    coarse_part(2.0 * q, tr_ref, pt_ref, ept_ref, w_refs, me, sh, t_scr)
    mine = pl.ds(pl.multiple_of(me * sh.piece, 16), sh.piece)
    own_r = state_ref[0, mine, :]
    send_t(
        t_scr,
        {
            0: total(state_ref[3, mine, :] * q),
            1: total(state_ref[1, mine, :] * q),
            2: total(own_r * own_r),
        },
        sh,
        t_out,
    )


def square_kernel(sh, place_ref, jump_ref, q0, q1, t_in, applied_out, t_out):
    me = place_ref[0]
    applied_out[...] = select_dot(jump_ref[...], jnp.concatenate([q0[...], q1[...]], axis=0))
    at = pl.multiple_of(me * sh.piece, 16)
    mine = applied_out[pl.ds(at, sh.piece), :]
    payload = jnp.where(sh.scalar_at(3), total(mine * mine), t_in[...])
    for i in range(sh.ndev):
        t_out[i] = payload


def third_kernel(
    sh, place_ref, tr_ref, pt_ref, ep_ref, ept_ref, applied_ref, t_in, w0, w1, tr0_ref,
    state_ref, lam_ref, ops_ref,
    next_out, tr1_out, q_out, t_out, t_scr, jd_scr,
):
    me = place_ref[0]
    w_refs = (w0, w1)
    sums = sum_parcels(t_in, sh)
    tr0 = tr0_ref[...]
    d_a, r_a, r_r, a_a = (pick(sums, sh, i) for i in range(4))
    rw0 = r_r - norm2(tr0, sh)
    alpha = rw0 / d_a
    tr1 = tr0 - alpha * sums
    rw1 = (r_r - 2.0 * alpha * r_a + alpha * alpha * a_a) - norm2(tr1, sh)
    beta = rw1 / rw0
    tr1_out[...] = jnp.where(sh.scalar_at(0), rw1, tr1)
    back = lift(tr_ref, pt_ref, ep_ref, w_refs, tr1_out, me, sh)
    applied = applied_ref[...]
    direction = state_ref[2]
    jump_d = (state_ref[1] - 2.0 * alpha * applied - 2.0 * back) + beta * state_ref[3]
    jd_scr[...] = jump_d
    residual = state_ref[0] - alpha * applied
    next_out[0] = residual
    next_out[1] = (residual - back) + beta * direction
    next_out[2] = lam_ref[...] + alpha * direction
    q = product(lanes_of(jump_d, sh).astype(BF16), ops_ref, sh)
    q_out[...] = q
    coarse_part(2.0 * q, tr_ref, pt_ref, ept_ref, w_refs, me, sh, t_scr)
    at = pl.multiple_of(me * sh.piece, 16)
    send_t(t_scr, {0: total(jd_scr[pl.ds(at, sh.piece), :] * q)}, sh, t_out)


def last_kernel(
    sh, place_ref, tr_ref, pt_ref, jump_ref, ep_ref, q0, q1, t_in, w0, w1, tr1_ref, state_ref,
    lam_out, p_out, t_scr,
):
    me = place_ref[0]
    sums = sum_parcels(t_in, sh)
    tr1 = tr1_ref[...]
    alpha = pick(tr1, sh, 0) / pick(sums, sh, 0)
    t_scr[...] = tr1 - alpha * sums
    applied = select_dot(jump_ref[...], jnp.concatenate([q0[...], q1[...]], axis=0))
    back = lift(tr_ref, pt_ref, ep_ref, (w0, w1), t_scr, me, sh)
    lam = state_ref[2] + alpha * state_ref[1]
    projected = (state_ref[0] - alpha * applied) - back
    lam_out[...] = lanes_of(lam, sh)[: sh.subs]
    p_out[...] = lanes_of(projected, sh)[: sh.subs]


def permute(value, move):
    sub_num, crs_num = lax.axis_size("sub"), lax.axis_size("crs")
    pairs = []
    for i in range(sub_num):
        for j in range(crs_num):
            to_i, to_j = move(i, j)
            if 0 <= to_i < sub_num:
                pairs.append((i * crs_num + j, to_i * crs_num + to_j))
    return lax.ppermute(value, AXES, pairs)


def swap_a(value):
    return permute(value, lambda i, j: (i ^ 1, j))


def swap_b(value):
    return permute(value, lambda i, j: (((i + 1) ^ 1) - 1, j))


def core_swap(value):
    return permute(value, lambda i, j: (i, j ^ 1))


def x_swaps(value):
    return [
        permute(value, lambda i, j: (i, j ^ (2 * shift)))
        for shift in range(1, lax.axis_size("crs") // 2)
    ]


def spread_pieces(value):
    near = jnp.concatenate([value, swap_a(value), swap_b(value)], axis=0)
    first = jnp.concatenate([near] + x_swaps(near), axis=0)
    return first, core_swap(first)


def local(
    dual_ops, rigid_traces, coarse_factor, partner, send_list, mode_count, dual_rhs, rigid_load
):
    sh = Shape(dual_ops, rigid_traces, coarse_factor, partner, send_list)
    modes, subs = sh.modes, sh.subs
    place = jnp.stack([lax.axis_index("crs"), lax.axis_index("sub") % 2]).astype(jnp.int32)

    vmem = pl.BlockSpec(memory_space=pltpu.VMEM)
    smem = pl.BlockSpec(memory_space=pltpu.SMEM)
    hbm = pl.BlockSpec(memory_space=pltpu.HBM)

    tags = {"v": vmem, "k": vmem, "s": smem, "h": hbm}

    def call(kernel, ins, outs, scratch, *operands, name, cost):
        operands = [
            pltpu.with_memory_space_constraint(x, pltpu.HBM) if tag == "h" else x
            for tag, x in zip(ins, operands)
        ]
        return pl.pallas_call(
            functools.partial(kernel, sh),
            out_shape=[
                pltpu.VMEM(s, t) if tag == "k" else jax.ShapeDtypeStruct(s, t)
                for tag, s, t in outs
            ],
            in_specs=[smem] + [tags[tag] for tag in ins],
            out_specs=[tags[tag] for tag, _, _ in outs],
            scratch_shapes=scratch,
            compiler_params=pltpu.CompilerParams(vmem_limit_bytes=24 * 1024 * 1024),
            cost_estimate=pl.CostEstimate(flops=0, bytes_accessed=cost, transcendentals=0),
            name=name,
        )(place, *operands)

    rows = (sh.all_rows, LANES)
    t_shape = ("v", (sh.t_rows, LANES), F32)
    parcels = ("v", (sh.ndev, sh.t_rows, LANES), F32)
    columns = ("v", (sh.sum_rows, LANES), F32)
    q_shape = ("v", (sh.piece, LANES), F32)
    field_shape = ("v", (modes + 1,) + rows, F32)
    t_scratch = pltpu.VMEM((sh.t_rows, LANES), F32)
    ops = dual_ops.reshape(subs * sh.rows, sh.order)
    ops_kept = ("k", ops.shape, BF16)
    ops_sems = subs // sh.group
    long = dual_ops.size * 2

    def exchange(parcel):
        return lax.all_to_all(parcel, AXES, 0, 0)

    def stack(count):
        return (count,) + rows

    parcel_shape = ("v", (sh.parcel + sh.factor_rows, LANES), F32)
    load = rigid_load[None, :]
    (t_part,) = call(
        start_kernel, "shh", [columns],
        [pltpu.VMEM(load.shape, F32), pltpu.VMEM(coarse_factor.shape, F32)]
        + [pltpu.SemaphoreType.DMA((2,))],
        mode_count, load, coarse_factor, name="start", cost=100_000,
    )
    t_sum = t_part + permute(t_part, lambda i, j: (i ^ 1, j))
    raw = (rigid_traces, dual_rhs, send_list, coarse_factor)
    fields, parcel_a, parcel_b, factor = call(
        pack_kernel, "shhhhv",
        [field_shape, parcel_shape, parcel_shape, ("v", (sh.factor_rows, LANES), F32)],
        [pltpu.VMEM((sh.slot_lanes, LANES), F32)]
        + [pltpu.VMEM(x.shape, x.dtype) for x in raw]
        + [pltpu.SemaphoreType.DMA((len(raw),))],
        mode_count, *raw, t_part, name="pack", cost=8_000_000,
    )
    parcel_a, parcel_b, factor, t_sum = lax.optimization_barrier(
        (parcel_a, parcel_b, factor, t_sum)
    )
    near_a, near_b = swap_a(parcel_a), swap_b(parcel_b)
    factor_x = x_swaps(factor)
    sum_steps = [2**k for k in range(1, (lax.axis_size("sub") - 1).bit_length())]
    for step in sum_steps[:-1]:
        t_sum = t_sum + permute(t_sum, lambda i, j: (i ^ step, j))
    ops_vmem, t_same = call(
        load_kernel, "hv", [ops_kept, columns], [pltpu.SemaphoreType.DMA((ops_sems,))],
        ops, t_sum, name="load", cost=long,
    )
    for step in sum_steps[-1:]:
        t_same = t_same + permute(t_sum, lambda i, j: (i ^ step, j))
    t_sum = t_same

    halves = core_swap(jnp.concatenate([near_a[: sh.names_at], near_b[: sh.names_at]], axis=0))
    factor_ab = jnp.concatenate([near_a[sh.parcel :], near_b[sh.parcel :], t_sum], axis=0)
    pair_rows = 2 * sh.factor_rows
    w0, sums = [factor, factor_ab[:pair_rows]], [t_sum]
    for own, pair in zip(factor_x, x_swaps(factor_ab)):
        w0 += [own, pair[:pair_rows]]
        sums.append(pair[pair_rows:])
    traces, far_traces, jumper, far_pick, far_put = call(
        setup_kernel, "vvvvv",
        [
            field_shape, field_shape,
            ("v", (sh.all_rows, 3 * sh.crs * sh.piece), BF16),
            ("v", (sh.all_rows, 3 * sh.pad), BF16),
            ("v", (3 * sh.pad, sh.piece), BF16),
        ],
        [pltpu.VMEM(rows, F32)],
        partner, fields, near_a, near_b, halves, name="setup", cost=6_000_000,
    )
    w0 = jnp.concatenate(w0 + sums + [far_traces[0, :8]], axis=0)
    w1 = core_swap(w0)
    lam0, q, t_part = call(
        first_kernel, "vvvvvvv",
        [("v", rows, F32), q_shape, parcels],
        [t_scratch],
        traces, far_traces, far_pick, far_put, w0, w1, ops_vmem, name="first", cost=long,
    )
    q0, q1 = spread_pieces(q)
    t_in = exchange(t_part)

    state0, tr0, q, t_part, ops_vmem = call(
        second_kernel, "vvvvvvvvvvh",
        [("v", stack(4), F32), t_shape, q_shape, t_shape, ops_kept],
        [t_scratch, pltpu.SemaphoreType.DMA((ops_sems,))],
        traces, far_traces, jumper, far_pick, far_put, q0, q1, t_in, w0, w1, ops,
        name="second", cost=long,
    )
    q0, q1 = spread_pieces(q)
    applied, t_part = call(
        square_kernel, "vvvv", [("v", rows, F32), parcels], [],
        jumper, q0, q1, t_part, name="square", cost=2_000_000,
    )
    t_in = exchange(t_part)

    state1, tr1, q, t_part = call(
        third_kernel, "vvvvvvvvvvvv",
        [("v", stack(3), F32), t_shape, q_shape, parcels],
        [t_scratch, pltpu.VMEM(rows, F32)],
        traces, far_traces, far_pick, far_put, applied, t_in, w0, w1, tr0, state0, lam0, ops_vmem,
        name="third", cost=long,
    )
    q0, q1 = spread_pieces(q)
    t_in = exchange(t_part)

    return tuple(
        call(
            last_kernel, "vvvvvvvvvvv",
            [("v", (subs, sh.order), F32)] * 2,
            [t_scratch],
            traces, far_traces, jumper, far_pick, q0, q1, t_in, w0, w1, tr1, state1,
            name="last", cost=4_000_000,
        )
    )


def body(*args):
    dual_ops, _, _, partner = args[:4]
    crs_num, sub_num = lax.axis_size("crs"), lax.axis_size("sub")
    whole_blocks = (
        dual_ops.shape[2] // partner.shape[1] == LANES and dual_ops.shape[1] % LANES == 0
    )
    fits = whole_blocks and args[2].shape[1] % LANES + 8 <= LANES
    fits = fits and sub_num & (sub_num - 1) == 0
    if fits and crs_num % 2 == 0 and crs_num & (crs_num - 1) == 0 and sub_num % 2 == 0:
        return local(*args)
    return plain(*args)


def solution(mesh):
    return jax.shard_map(
        body,
        mesh=mesh,
        in_specs=(
            P("sub", "crs", None),
            P("sub", None, None),
            P("sub", "crs"),
            P("sub", None),
            P("sub", None),
            P("sub"),
            P("sub", None),
            P("sub"),
        ),
        out_specs=(P("sub", None), P("sub", None)),
        check_vma=False,
    )
```

```python
import functools

import jax
import jax.numpy as jnp
from jax import lax
from jax.experimental import pallas as pl
from jax.experimental.pallas import tpu as pltpu
from jax.sharding import PartitionSpec as P

ITERATIONS = 2
AXES = ("sub", "crs")
LANES = 128
F32 = jnp.float32
BF16 = jnp.bfloat16


def with_halo(block, sides, width):
    for axis, dim in sides:
        count = lax.axis_size(axis)
        forward = [(i, i + 1) for i in range(count - 1)]
        backward = [(target, source) for source, target in forward]
        low = lax.ppermute(
            lax.slice_in_dim(block, block.shape[dim] - width, None, axis=dim), axis, forward
        )
        high = lax.ppermute(lax.slice_in_dim(block, 0, width, axis=dim), axis, backward)
        block = jnp.concatenate([low, block, high], axis=dim)
    return block


def plain(
    dual_ops, rigid_traces, coarse_factor, partner, send_list, mode_count, dual_rhs, rigid_load
):
    sub_count = dual_ops.shape[0]
    block_num = partner.shape[1]
    order_len = dual_ops.shape[2]
    block_len = order_len // block_num
    local_blocks = sub_count * block_num
    mode_num = rigid_traces.shape[1]
    links = partner.reshape(local_blocks)
    linked = (links >= 0)[:, None]
    source = jnp.maximum(links, 0)
    sending = (send_list >= 0)[:, :, None]
    picked = jnp.maximum(send_list, 0)
    mode_mask = (jnp.arange(mode_num, dtype=jnp.int32)[None, :] < mode_count[:, None]).astype(F32)

    def jump(vector):
        pieces = vector.reshape(local_blocks, block_len)
        parcels = jnp.where(sending, pieces[picked], 0.0)
        arrived = with_halo(parcels, (("sub", 0),), 1)
        incoming = jnp.concatenate([arrived[0], arrived[3]], axis=0)
        gathered = jnp.concatenate([pieces, incoming], axis=0)
        return jnp.where(linked, pieces - gathered[source], 0.0).reshape(vector.shape)

    def operator(vector):
        lowered = jump(vector).astype(BF16)
        partial_rows = jnp.einsum("srk,sk->sr", dual_ops, lowered, preferred_element_type=F32)
        full_rows = lax.all_gather(partial_rows, "crs", axis=1, tiled=True)
        return jump(full_rows)

    def restrict(vector):
        traced = jnp.einsum(
            "skm,sm->sk", rigid_traces, jump(vector), precision=lax.Precision.HIGHEST
        )
        return (traced * mode_mask).reshape(sub_count * mode_num)

    def expand(coarse_vec):
        scaled = coarse_vec.reshape(sub_count, mode_num) * mode_mask
        spread = jnp.einsum("skm,sk->sm", rigid_traces, scaled, precision=lax.Precision.HIGHEST)
        return jump(spread)

    def coarse(restricted, squares):
        column_part = jnp.dot(restricted, coarse_factor, precision=lax.Precision.HIGHEST)
        column_sum, total_sq = lax.psum((column_part, squares), "sub")
        back_part = jnp.dot(coarse_factor, column_sum, precision=lax.Precision.HIGHEST)
        solved, folded = lax.psum((back_part, jnp.sum(column_sum * column_sum)), "crs")
        return (solved, total_sq, folded)

    def project(residual):
        solved, total_sq, folded = coarse(restrict(residual), jnp.sum(residual * residual))
        return (residual - expand(solved), total_sq - folded)

    start_load = rigid_load * mode_mask.reshape(sub_count * mode_num)
    start_solved, _, _ = coarse(start_load, jnp.zeros((), F32))
    multipliers = expand(start_solved)
    residual = dual_rhs - operator(multipliers)
    projected, inner_rw = project(residual)
    direction = projected
    for _ in range(ITERATIONS):
        applied = operator(direction)
        curvature = lax.psum(jnp.sum(direction * applied), "sub")
        step_len = inner_rw / curvature
        multipliers = multipliers + step_len * direction
        residual = residual - step_len * applied
        projected, next_rw = project(residual)
        direction = projected + next_rw / inner_rw * direction
        inner_rw = next_rw
    return (multipliers, projected)


def split3(value):
    high = value.astype(BF16)
    rest = value - high.astype(F32)
    mid = rest.astype(BF16)
    low = (rest - mid.astype(F32)).astype(BF16)
    return high, mid, low


def select_dot(chooser, value):
    width = value.shape[1]
    wide = jnp.dot(
        chooser, jnp.concatenate(split3(value), axis=1), preferred_element_type=F32
    )
    return (wide[:, 2 * width :] + wide[:, width : 2 * width]) + wide[:, :width]


def one_hot(column, width):
    rows = column.shape[0]
    return (lax.broadcasted_iota(jnp.int32, (rows, width), 1) == column).astype(F32)


def repeated_one_hot(code, width):
    lane = lax.broadcasted_iota(jnp.int32, code.shape, 1)
    tiles = [(lane + at == code).astype(F32) for at in range(0, width, LANES)]
    return jnp.concatenate(tiles, axis=1)[:, :width].astype(BF16)


def floor_div(value, by, most):
    out = jnp.zeros(value.shape, jnp.int32)
    for i in range(1, most):
        out = out + (value >= i * by).astype(jnp.int32)
    return out


def total(value):
    return jnp.sum(jnp.sum(value, axis=0, keepdims=True), axis=1, keepdims=True)


class Shape:
    def __init__(self, dual_ops, rigid_traces, coarse_factor, partner, send_list):
        self.subs, self.rows, self.order = dual_ops.shape
        self.blocks = partner.shape[1]
        self.modes = rigid_traces.shape[1]
        self.slots = send_list.shape[1]
        self.crs = lax.axis_size("crs")
        self.ndev = lax.axis_size("sub") * self.crs
        self.pad = -(-self.subs // 16) * 16
        self.all_rows = self.blocks * self.pad
        self.piece_blocks = self.rows // LANES
        self.piece = self.piece_blocks * self.pad
        self.half_slots = -(-self.slots // 16) * 8
        self.planes = self.modes + 1
        self.group = 2 if self.subs % 2 == 0 else 1
        self.names_at = self.planes * self.half_slots
        self.slot_lanes = -(-2 * self.half_slots // LANES) * LANES
        self.parcel = self.names_at + 8 * (self.slot_lanes // LANES)
        self.cols = coarse_factor.shape[1]
        self.full = self.cols // LANES
        self.spot = self.cols % LANES
        self.halves = self.full + 1
        self.wide = self.halves * LANES
        self.t_rows = self.crs * self.halves
        self.row_sums = -(-self.t_rows // 8) * 8
        self.sum_rows = -(-self.halves // 8) * 8
        self.tile_rows = self.modes * self.pad
        self.beside = LANES // max(self.spot, 1)
        self.rest_tiles = -(-self.modes // self.beside) if self.spot else 0
        self.factor_rows = self.full * self.tile_rows + self.rest_tiles * self.pad

    def scalar_at(self, index):
        rows = lax.broadcasted_iota(jnp.int32, (self.t_rows, LANES), 0)
        lanes = lax.broadcasted_iota(jnp.int32, (self.t_rows, LANES), 1)
        return (rows == self.halves - 1) & (lanes == self.spot + index)

    def t_mask(self):
        rows = lax.broadcasted_iota(jnp.int32, (self.t_rows, LANES), 0)
        lanes = lax.broadcasted_iota(jnp.int32, (self.t_rows, LANES), 1)
        return (rows % self.halves < self.halves - 1) | (lanes < self.spot)

    def slot_of(self, rel):
        return (rel % 2) * (self.crs // 2) + rel // 2


def rows_of(value, sh):
    return jnp.concatenate(
        [value[:, b * LANES : (b + 1) * LANES] for b in range(value.shape[1] // LANES)], axis=0
    )


def rows_of_lanes(value):
    return jnp.concatenate(
        [value[:, at : at + LANES] for at in range(0, value.shape[1], LANES)], axis=0
    )


def lanes_of(value, sh):
    return jnp.concatenate(
        [value[b * sh.pad : (b + 1) * sh.pad] for b in range(value.shape[0] // sh.pad)], axis=1
    )


def factor_tile(w_refs, sh, rel, where, at):
    slot = sh.slot_of(rel)
    xs = sh.crs // 2
    base = ((slot % xs) * 3 + where) * sh.factor_rows + at
    return w_refs[slot // xs][base : base + sh.pad, :]


def full_tile(w_refs, sh, rel, where, mode, h):
    return factor_tile(w_refs, sh, rel, where, h * sh.tile_rows + mode * sh.pad)


def rest_tile(w_refs, sh, rel, where, tile):
    return factor_tile(w_refs, sh, rel, where, sh.full * sh.tile_rows + tile * sh.pad)


def lane_group(sh, shape):
    lane = lax.broadcasted_iota(jnp.int32, shape, 1)
    return floor_div(lane, sh.spot, sh.beside + 1)


def coarse_back(w_refs, t_ref, me, sh):
    t_row, t_rest = {}, []
    lane = lax.broadcasted_iota(jnp.int32, (8, LANES), 1)
    for rel in range(sh.crs):
        at = jnp.bitwise_xor(me, rel) * sh.halves
        for h in range(sh.full):
            t_row[rel, h] = t_ref[pl.ds(at + h, 1), :]
        if sh.spot:
            rest = jnp.broadcast_to(t_ref[pl.ds(at + sh.full, 1), :], (8, LANES))
            rest = jnp.where(lane < sh.spot, rest, 0.0)
            spread = rest
            for i in range(1, sh.beside):
                spread = spread + pltpu.roll(rest, i * sh.spot, 1)
            t_rest.append(spread[:1])
    rests = {}
    for where in range(3):
        for tile in range(sh.rest_tiles):
            acc = jnp.zeros((sh.pad, LANES), F32)
            for rel in range(sh.crs):
                acc += rest_tile(w_refs, sh, rel, where, tile) * t_rest[rel]
            rests[where, tile] = acc
    group = lane_group(sh, (sh.pad, LANES)) if sh.spot else None
    lanes = lax.broadcasted_iota(jnp.int32, (sh.pad, LANES), 1)
    parts = [jnp.zeros((sh.pad, LANES), F32)] * 3
    for mode in range(sh.modes):
        for where in range(3):
            acc = jnp.zeros((sh.pad, LANES), F32)
            if sh.spot:
                mine = group == mode % sh.beside
                acc = jnp.where(mine, rests[where, mode // sh.beside], 0.0)
            for rel in range(sh.crs):
                for h in range(sh.full):
                    acc += full_tile(w_refs, sh, rel, where, mode, h) * t_row[rel, h]
            parts[where] = jnp.where(
                lanes == mode, jnp.sum(acc, axis=1, keepdims=True), parts[where]
            )
    return jnp.concatenate(parts, axis=0)


def lift(tr_ref, pt_ref, ep_ref, w_refs, t_ref, me, sh):
    found = coarse_back(w_refs, t_ref, me, sh)
    far = select_dot(ep_ref[...], found)
    out = jnp.zeros((sh.all_rows, LANES), F32)
    for mode in range(sh.modes):
        own = jnp.broadcast_to(found[: sh.pad, mode : mode + 1], (sh.pad, LANES))
        own = jnp.concatenate([own] * sh.blocks, axis=0)
        out += tr_ref[mode] * own - pt_ref[mode] * far[:, mode : mode + 1]
    return out


def coarse_part(value, tr_ref, pt_ref, ept_ref, w_refs, me, sh, t_out):
    at = pl.multiple_of(me * sh.piece, 16)
    lanes = lax.broadcasted_iota(jnp.int32, (sh.piece, LANES), 1)
    own, far = [], jnp.zeros((sh.piece, LANES), F32)
    for mode in range(sh.modes):
        mine = tr_ref[mode, pl.ds(at, sh.piece), :] * value
        acc = mine[: sh.pad]
        for b in range(1, sh.piece_blocks):
            acc = acc + mine[b * sh.pad : (b + 1) * sh.pad]
        own.append(jnp.sum(acc, axis=1, keepdims=True))
        theirs = pt_ref[mode, pl.ds(at, sh.piece), :] * value
        far = jnp.where(lanes == mode, jnp.sum(theirs, axis=1, keepdims=True), far)
    moved = select_dot(ept_ref[...], far)
    sums, rests = {}, {}
    group = lane_group(sh, (sh.pad, LANES)) if sh.spot else None
    side = {}

    def add(table, key, term):
        table[key] = table[key] + term if key in table else term

    for mode in range(sh.modes):
        for where in range(3):
            weight = -moved[where * sh.pad : (where + 1) * sh.pad, mode : mode + 1]
            if where == 0:
                weight = weight + own[mode]
            weight = jnp.broadcast_to(weight, (sh.pad, LANES))
            for rel in range(sh.crs):
                for h in range(sh.full):
                    add(sums, (rel, h), full_tile(w_refs, sh, rel, where, mode, h) * weight)
            if sh.spot:
                mine = group == mode % sh.beside
                add(side, (where, mode // sh.beside), jnp.where(mine, weight, 0.0))
    for (where, tile), weight in side.items():
        for rel in range(sh.crs):
            add(rests, rel, rest_tile(w_refs, sh, rel, where, tile) * weight)
    for rel in range(sh.crs):
        at_t = jnp.bitwise_xor(me, rel) * sh.halves
        for h in range(sh.full):
            t_out[pl.ds(at_t + h, 1), :] = jnp.sum(sums[rel, h], axis=0, keepdims=True)
        last = jnp.zeros((1, LANES), F32)
        if sh.spot:
            row = jnp.broadcast_to(jnp.sum(rests[rel], axis=0, keepdims=True), (8, LANES))
            folded = row
            for i in range(1, min(sh.beside, sh.modes)):
                folded = folded + pltpu.roll(row, LANES - i * sh.spot, 1)
            last = folded[:1]
        t_out[pl.ds(at_t + sh.full, 1), :] = last


def ops_copies(ops_hbm, ops_vmem, sems, sh):
    span = sh.group * sh.rows
    return [
        pltpu.make_async_copy(
            ops_hbm.at[pl.ds(i * span, span)], ops_vmem.at[pl.ds(i * span, span)], sems.at[i]
        )
        for i in range(sh.subs // sh.group)
    ]


def product(lowered, ops_vmem, sh, copies=None):
    row = lax.broadcasted_iota(jnp.int32, (sh.pad, sh.rows), 0)
    acc = jnp.zeros((sh.pad, sh.rows), F32)
    wide = lowered.astype(F32)
    for s in range(sh.subs):
        if copies is not None and s % sh.group == 0:
            copies[s // sh.group].wait()
        base = s * sh.rows
        if s % 2 == 0:
            part = lax.dot_general(
                lowered,
                ops_vmem[base : base + sh.rows],
                (((1,), (1,)), ((), ())),
                preferred_element_type=F32,
            )
        else:
            sums = []
            for at in range(base, base + sh.rows, LANES):
                tile = jnp.zeros((LANES, LANES), F32)
                for k in range(0, sh.order, LANES):
                    block = ops_vmem[at : at + LANES, k : k + LANES].astype(F32)
                    tile = tile + block * wide[s : s + 1, k : k + LANES]
                sums.append(jnp.sum(jnp.transpose(tile), axis=0, keepdims=True))
            part = jnp.concatenate(sums, axis=1)
        acc = jnp.where(row == s, part, acc)
    return rows_of(acc, sh)


def sum_parcels(t_in_ref):
    acc = t_in_ref[0]
    for i in range(1, t_in_ref.shape[0]):
        acc = acc + t_in_ref[i]
    return acc


def pick(t_sum, sh, index):
    return total(jnp.where(sh.scalar_at(index), t_sum, 0.0))


def norm2(t_vec, sh):
    return total(jnp.where(sh.t_mask(), t_vec * t_vec, 0.0))


def send_t(t_scr, scalars, sh, t_out):
    payload = jnp.where(sh.t_mask(), t_scr[...], 0.0)
    for index, value in scalars.items():
        payload = jnp.where(sh.scalar_at(index), value, payload)
    if len(t_out.shape) == 2:
        t_out[...] = payload
    else:
        for i in range(sh.ndev):
            t_out[i] = payload


def start_kernel(sh, place_ref, count_ref, load_hbm, factor_hbm, t_out, load_ref, factor_ref, sems):
    copies = [
        pltpu.make_async_copy(load_hbm, load_ref, sems.at[0]),
        pltpu.make_async_copy(factor_hbm, factor_ref, sems.at[1]),
    ]
    for copy in copies:
        copy.start()
    for copy in copies:
        copy.wait()
    lane = lax.broadcasted_iota(jnp.int32, (8, sh.subs * sh.modes), 1)
    kept = lane < 0
    for s in range(sh.subs):
        kept = kept | ((lane >= s * sh.modes) & (lane < s * sh.modes + count_ref[s]))
    load = jnp.where(kept, jnp.broadcast_to(load_ref[...], kept.shape), 0.0)
    part = jnp.dot(
        load, factor_ref[...], preferred_element_type=F32, precision=lax.Precision.HIGHEST
    )
    part = jnp.concatenate([part, jnp.zeros((8, sh.wide - sh.cols), F32)], axis=1)[:1]
    part = rows_of_lanes(part)
    empty = jnp.zeros((sh.sum_rows - sh.halves, LANES), F32)
    t_out[...] = jnp.concatenate([part, empty], axis=0)


def load_kernel(sh, place_ref, ops_hbm, sum_ref, ops_out, sum_out, sems):
    copies = ops_copies(ops_hbm, ops_out, sems, sh)
    for copy in copies:
        copy.start()
    sum_out[...] = sum_ref[...]
    for copy in copies:
        copy.wait()


def pack_kernel(
    sh, place_ref, count_ref, traces_hbm, rhs_hbm, send_hbm, factor_hbm, after_ref,
    fields_out, parcel_a, parcel_b, factor_out,
    slot_scr, traces_ref, rhs_ref, send_ref, factor_ref, sems,
):
    copies = [
        pltpu.make_async_copy(source, target, sems.at[i])
        for i, (source, target) in enumerate(
            (
                (factor_hbm, factor_ref),
                (send_hbm, send_ref),
                (rhs_hbm, rhs_ref),
                (traces_hbm, traces_ref),
            )
        )
    ]
    for copy in copies:
        copy.start()
    for copy in copies:
        copy.wait()
    me, odd = place_ref[0], place_ref[1]
    group = -(-(sh.modes + 1) // 8) * 8
    filler = jnp.zeros((group - sh.modes - 1, sh.order), F32)
    row = lax.broadcasted_iota(jnp.int32, (group, sh.order), 0)
    tiles = []
    for s in range(sh.subs):
        tile = jnp.concatenate([traces_ref[s], rhs_ref[s : s + 1, :], filler], axis=0)
        tiles.append(jnp.where((row < count_ref[s]) | (row >= sh.modes), tile, 0.0))
    by_sub = jnp.concatenate(tiles, axis=0)
    shape = ((sh.modes + 1) * sh.pad, sh.subs * group)
    out_row = lax.broadcasted_iota(jnp.int32, shape, 0)
    mode = floor_div(out_row, sh.pad, sh.modes + 1)
    sub = out_row - mode * sh.pad
    hit = lax.broadcasted_iota(jnp.int32, shape, 1) == sub * group + mode
    order = jnp.where(hit & (sub < sh.subs), 1.0, 0.0).astype(BF16)
    by_mode = select_dot(order, by_sub)
    fields = []
    for k in range(sh.modes + 1):
        fields.append(rows_of(by_mode[k * sh.pad : (k + 1) * sh.pad], sh))
        fields_out[k] = fields[k]
    fields = jnp.concatenate(fields, axis=1)

    shape = (sh.tile_rows, sh.subs * sh.modes)
    out_row = lax.broadcasted_iota(jnp.int32, shape, 0)
    mode = floor_div(out_row, sh.pad, sh.modes)
    sub = out_row - mode * sh.pad
    hit = lax.broadcasted_iota(jnp.int32, shape, 1) == sub * sh.modes + mode
    order = jnp.where(hit & (sub < sh.subs), 1.0, 0.0).astype(BF16)
    factor = select_dot(order, factor_ref[...])
    factor = jnp.concatenate(
        [factor, jnp.zeros((sh.tile_rows, sh.wide - sh.cols), F32)], axis=1
    )
    tiles = [factor[:, h * LANES : (h + 1) * LANES] for h in range(sh.full)]
    rest = factor[:, sh.full * LANES :]
    for tile in range(sh.rest_tiles):
        side = jnp.zeros((sh.pad, LANES), F32)
        for i in range(min(sh.beside, sh.modes - tile * sh.beside)):
            mode = tile * sh.beside + i
            part = rest[mode * sh.pad : (mode + 1) * sh.pad]
            side = side + (pltpu.roll(part, i * sh.spot, 1) if i else part)
        tiles.append(side)
    factor = jnp.concatenate(tiles, axis=0)
    factor_out[...] = factor

    width = sh.slot_lanes
    lists = send_ref[...].astype(F32)
    lists = jnp.concatenate([lists, jnp.full((2, width - sh.slots), -1.0, F32)], axis=1)
    lists = jnp.concatenate([lists, jnp.full((6, width), -1.0, F32)], axis=0).astype(jnp.int32)
    sub = floor_div(lists, sh.blocks, sh.subs)
    lists = jnp.where(lists >= 0, (lists - sub * sh.blocks) * sh.pad + sub, -1).astype(F32)
    turned = jnp.transpose(lists)
    at = pl.multiple_of((me % 2) * sh.half_slots, 8)
    for out, row in ((parcel_a, 1 - odd), (parcel_b, odd)):
        names = jnp.where(row == 0, lists[0:1], lists[1:2])
        column = jnp.where(row == 0, turned[:, 0:1], turned[:, 1:2])
        slot_scr[...] = jnp.broadcast_to(column, (width, LANES))
        line = slot_scr[pl.ds(at, sh.half_slots), :].astype(jnp.int32)
        picked = select_dot(repeated_one_hot(line, sh.all_rows), fields)
        for k in range(sh.planes):
            out[k * sh.half_slots : (k + 1) * sh.half_slots, :] = picked[
                :, k * LANES : (k + 1) * LANES
            ]
        for i in range(width // LANES):
            out[sh.names_at + 8 * i : sh.names_at + 8 * (i + 1), :] = jnp.broadcast_to(
                names[:, i * LANES : (i + 1) * LANES], (8, LANES)
            )
        out[sh.parcel :, :] = factor


def setup_kernel(
    sh, place_ref, partner_ref, fields_ref, near_a, near_b, core_ref,
    tr_out, pt_out, jump_out, ep_out, ept_out, sub_scr,
):
    me, odd = place_ref[0], place_ref[1]
    codes = partner_ref[...]
    codes = jnp.concatenate(
        [codes, jnp.full((sh.pad - sh.subs, sh.blocks), -1, jnp.int32)], axis=0
    )
    code = jnp.concatenate(
        [jnp.broadcast_to(codes[:, b : b + 1], (sh.pad, LANES)) for b in range(sh.blocks)], axis=0
    )
    local_blocks = sh.subs * sh.blocks
    linked = code >= 0
    is_own = linked & (code < local_blocks)
    before = (code >= local_blocks) & (code < local_blocks + sh.slots)
    after = code >= local_blocks + sh.slots
    is_a = (before & (odd == 1)) | (after & (odd == 0))
    slot = jnp.where(before, code - local_blocks, code - local_blocks - sh.slots)
    upper = (slot >= sh.half_slots).astype(jnp.int32)
    other = jnp.where(upper == me % 2, 0, 1)
    own_sub = floor_div(code, sh.blocks, sh.subs)
    line = (code - own_sub * sh.blocks) * sh.pad + own_sub
    source = jnp.where(
        is_own,
        line,
        sh.all_rows
        + other * 2 * sh.half_slots
        + jnp.where(is_a, 0, sh.half_slots)
        + (slot - upper * sh.half_slots),
    )
    source = jnp.where(linked, source, -1)
    chooser = repeated_one_hot(source, sh.all_rows + 4 * sh.half_slots)
    columns = []
    for k in range(sh.planes):
        rows = slice(k * sh.half_slots, (k + 1) * sh.half_slots)
        rows_b = slice(sh.names_at + k * sh.half_slots, sh.names_at + (k + 1) * sh.half_slots)
        columns.append(
            jnp.concatenate(
                [
                    fields_ref[k], near_a[rows, :], near_b[rows, :],
                    core_ref[rows, :], core_ref[rows_b, :],
                ],
                axis=0,
            )
        )
    far = select_dot(chooser, jnp.concatenate(columns, axis=1))
    live = linked.astype(F32)
    for k in range(sh.modes + 1):
        far_k = far[:, k * LANES : (k + 1) * LANES]
        if k < sh.modes:
            tr_out[k] = fields_ref[k] * live
            pt_out[k] = far_k
        else:
            tr_out[k] = fields_ref[k]
            pt_out[k] = fields_ref[k] * live - far_k

    names = []
    for ref in (near_a, near_b):
        parts = []
        for i in range(sh.slot_lanes // LANES):
            tile = ref[sh.names_at + 8 * i : sh.names_at + 8 * (i + 1), :]
            parts.append(jnp.broadcast_to(jnp.transpose(tile)[:, 0:1], (LANES, LANES)))
        names.append(jnp.concatenate(parts, axis=0))
    named = select_dot(
        repeated_one_hot(slot, sh.slot_lanes), jnp.concatenate(names, axis=1)
    ).astype(jnp.int32)
    far_line = jnp.where(is_own, line, jnp.where(is_a, named[:, :LANES], named[:, LANES:]))
    wide = (sh.all_rows, LANES)
    own_line = lax.broadcasted_iota(jnp.int32, wide, 0)

    def piece_row(block, sub, where):
        member = floor_div(block, sh.piece_blocks, sh.crs)
        place = sh.slot_of(jnp.bitwise_xor(member, me)) * 3 + where
        return place * sh.piece + (block - member * sh.piece_blocks) * sh.pad + sub

    def split(value):
        block = floor_div(value, sh.pad, sh.blocks)
        return block, value - block * sh.pad

    far_block, far_sub = split(far_line)
    own_block, own_sub = split(own_line)
    where = jnp.where(is_own, 0, jnp.where(is_a, 1, 2))
    own_col = jnp.where(linked, piece_row(own_block, own_sub, 0), -1)
    far_col = jnp.where(linked, piece_row(far_block, far_sub, where), -1)
    columns = 3 * sh.crs * sh.piece
    jump_out[...] = repeated_one_hot(own_col, columns) - repeated_one_hot(far_col, columns)
    far_sub = jnp.where(linked, where * sh.pad + far_sub, -1)
    pick_far = repeated_one_hot(far_sub, 3 * sh.pad)
    ep_out[...] = pick_far
    sub_scr[...] = far_sub.astype(F32)
    mine = sub_scr[pl.ds(pl.multiple_of(me * sh.piece, 16), sh.piece), :]
    mine = jnp.transpose(mine)[: 3 * sh.pad] if 3 * sh.pad <= LANES else jnp.transpose(mine)
    row = lax.broadcasted_iota(jnp.int32, (3 * sh.pad, sh.piece), 0).astype(F32)
    ept_out[...] = jnp.where(mine[:1] == row, 1.0, 0.0).astype(BF16)


def first_kernel(
    sh, place_ref, tr_ref, pt_ref, ep_ref, ept_ref, w0, w1, ops_ref,
    lam_out, q_out, t_out, t_scr,
):
    me = place_ref[0]
    w_refs = (w0, w1)
    for rel in range(sh.crs):
        at = jnp.bitwise_xor(me, rel) * sh.halves
        base = sh.crs // 2 * 3 * sh.factor_rows + rel // 2 * sh.sum_rows
        for h in range(sh.halves):
            t_scr[pl.ds(at + h, 1), :] = w_refs[rel % 2][base + h : base + h + 1, :]
    lam = lift(tr_ref, pt_ref, ep_ref, w_refs, t_scr, me, sh)
    lam_out[...] = lam
    q = product(lanes_of(2.0 * lam, sh).astype(BF16), ops_ref, sh)
    q_out[...] = q
    at = pl.multiple_of(me * sh.piece, 16)
    value = tr_ref[sh.modes, pl.ds(at, sh.piece), :] - 2.0 * q
    coarse_part(value, tr_ref, pt_ref, ept_ref, w_refs, me, sh, t_scr)
    send_t(t_scr, {}, sh, t_out)


def second_kernel(
    sh, place_ref, tr_ref, pt_ref, jump_ref, ep_ref, ept_ref, q0, q1, t_in, w0, w1, ops_hbm,
    state_ref, tr0_out, q_out, ops_out, t_scr, t_out, sems,
):
    copies = ops_copies(ops_hbm, ops_out, sems, sh)
    for copy in copies:
        copy.start()
    me = place_ref[0]
    w_refs = (w0, w1)
    applied = select_dot(jump_ref[...], jnp.concatenate([q0[...], q1[...]], axis=0))
    tr0_out[...] = sum_parcels(t_in)
    back = lift(tr_ref, pt_ref, ep_ref, w_refs, tr0_out, me, sh)
    residual = tr_ref[sh.modes] - applied
    jump_r = pt_ref[sh.modes] - 2.0 * applied
    jump_d = jump_r - 2.0 * back
    state_ref[0] = residual
    state_ref[1] = jump_r
    state_ref[2] = residual - back
    state_ref[3] = jump_d
    q = product(lanes_of(jump_d, sh).astype(BF16), ops_out, sh, copies)
    q_out[: sh.piece, :] = q
    coarse_part(2.0 * q, tr_ref, pt_ref, ept_ref, w_refs, me, sh, t_scr)
    mine = pl.ds(pl.multiple_of(me * sh.piece, 16), sh.piece)
    own_r = state_ref[0, mine, :]
    send_t(
        t_scr,
        {
            0: total(state_ref[3, mine, :] * q),
            1: total(state_ref[1, mine, :] * q),
            2: total(own_r * own_r),
        },
        sh,
        t_out,
    )
    filler = jnp.zeros((sh.row_sums - sh.t_rows, LANES), F32)
    q_out[sh.piece :, :] = jnp.concatenate([t_out[...], filler], axis=0) if (
        sh.row_sums > sh.t_rows
    ) else t_out[...]


def square_kernel(sh, place_ref, jump_ref, q0, q1, applied_out, t_out):
    span = sh.piece + sh.row_sums
    pieces, sums = [], jnp.zeros((sh.t_rows, LANES), F32)
    for ref in (q0, q1):
        for i in range(3 * sh.crs // 2):
            pieces.append(ref[i * span : i * span + sh.piece, :])
            if i % 3 == 0:
                sums = sums + ref[i * span + sh.piece : i * span + sh.piece + sh.t_rows, :]
    applied = select_dot(jump_ref[...], jnp.concatenate(pieces, axis=0))
    applied_out[...] = applied
    payload = jnp.where(sh.scalar_at(3), total(applied * applied), sums)
    for i in range(t_out.shape[0]):
        t_out[i] = payload


def third_kernel(
    sh, place_ref, tr_ref, pt_ref, ep_ref, ept_ref, applied_ref, t_in, w0, w1, tr0_ref,
    state_ref, lam_ref, ops_ref,
    next_out, tr1_out, q_out, t_out, t_scr, jd_scr,
):
    me = place_ref[0]
    w_refs = (w0, w1)
    sums = sum_parcels(t_in)
    tr0 = tr0_ref[...]
    d_a, r_a, r_r, a_a = (pick(sums, sh, i) for i in range(4))
    rw0 = r_r - norm2(tr0, sh)
    alpha = rw0 / d_a
    tr1 = tr0 - alpha * sums
    rw1 = (r_r - 2.0 * alpha * r_a + alpha * alpha * a_a) - norm2(tr1, sh)
    beta = rw1 / rw0
    tr1_out[...] = jnp.where(sh.scalar_at(0), rw1, tr1)
    back = lift(tr_ref, pt_ref, ep_ref, w_refs, tr1_out, me, sh)
    applied = applied_ref[...]
    direction = state_ref[2]
    jump_d = (state_ref[1] - 2.0 * alpha * applied - 2.0 * back) + beta * state_ref[3]
    jd_scr[...] = jump_d
    residual = state_ref[0] - alpha * applied
    next_out[0] = residual
    next_out[1] = (residual - back) + beta * direction
    next_out[2] = lam_ref[...] + alpha * direction
    q = product(lanes_of(jump_d, sh).astype(BF16), ops_ref, sh)
    q_out[...] = q
    coarse_part(2.0 * q, tr_ref, pt_ref, ept_ref, w_refs, me, sh, t_scr)
    at = pl.multiple_of(me * sh.piece, 16)
    send_t(t_scr, {0: total(jd_scr[pl.ds(at, sh.piece), :] * q)}, sh, t_out)


def last_kernel(
    sh, place_ref, tr_ref, pt_ref, jump_ref, ep_ref, q0, q1, t_in, w0, w1, tr1_ref, state_ref,
    lam_out, p_out, t_scr,
):
    me = place_ref[0]
    sums = sum_parcels(t_in)
    tr1 = tr1_ref[...]
    alpha = pick(tr1, sh, 0) / pick(sums, sh, 0)
    t_scr[...] = tr1 - alpha * sums
    applied = select_dot(jump_ref[...], jnp.concatenate([q0[...], q1[...]], axis=0))
    back = lift(tr_ref, pt_ref, ep_ref, (w0, w1), t_scr, me, sh)
    lam = state_ref[2] + alpha * state_ref[1]
    projected = (state_ref[0] - alpha * applied) - back
    lam_out[...] = lanes_of(lam, sh)[: sh.subs]
    p_out[...] = lanes_of(projected, sh)[: sh.subs]


def permute(value, move):
    sub_num, crs_num = lax.axis_size("sub"), lax.axis_size("crs")
    pairs = []
    for i in range(sub_num):
        for j in range(crs_num):
            to_i, to_j = move(i, j)
            if 0 <= to_i < sub_num:
                pairs.append((i * crs_num + j, to_i * crs_num + to_j))
    return lax.ppermute(value, AXES, pairs)


def swap_a(value):
    return permute(value, lambda i, j: (i ^ 1, j))


def swap_b(value):
    return permute(value, lambda i, j: (((i + 1) ^ 1) - 1, j))


def core_swap(value):
    return permute(value, lambda i, j: (i, j ^ 1))


def x_swaps(value):
    return [
        permute(value, lambda i, j: (i, j ^ (2 * shift)))
        for shift in range(1, lax.axis_size("crs") // 2)
    ]


def spread_pieces(value):
    near = jnp.concatenate([value, swap_a(value), swap_b(value)], axis=0)
    first = jnp.concatenate([near] + x_swaps(near), axis=0)
    return first, core_swap(first)


def local(
    dual_ops, rigid_traces, coarse_factor, partner, send_list, mode_count, dual_rhs, rigid_load
):
    sh = Shape(dual_ops, rigid_traces, coarse_factor, partner, send_list)
    modes, subs = sh.modes, sh.subs
    place = jnp.stack([lax.axis_index("crs"), lax.axis_index("sub") % 2]).astype(jnp.int32)

    vmem = pl.BlockSpec(memory_space=pltpu.VMEM)
    smem = pl.BlockSpec(memory_space=pltpu.SMEM)
    hbm = pl.BlockSpec(memory_space=pltpu.HBM)

    tags = {"v": vmem, "k": vmem, "s": smem, "h": hbm}

    def call(kernel, ins, outs, scratch, *operands, name, cost):
        operands = [
            pltpu.with_memory_space_constraint(x, pltpu.HBM) if tag == "h" else x
            for tag, x in zip(ins, operands)
        ]
        return pl.pallas_call(
            functools.partial(kernel, sh),
            out_shape=[
                pltpu.VMEM(s, t) if tag == "k" else jax.ShapeDtypeStruct(s, t)
                for tag, s, t in outs
            ],
            in_specs=[smem] + [tags[tag] for tag in ins],
            out_specs=[tags[tag] for tag, _, _ in outs],
            scratch_shapes=scratch,
            compiler_params=pltpu.CompilerParams(vmem_limit_bytes=24 * 1024 * 1024),
            cost_estimate=pl.CostEstimate(flops=0, bytes_accessed=cost, transcendentals=0),
            name=name,
        )(place, *operands)

    rows = (sh.all_rows, LANES)
    t_shape = ("v", (sh.t_rows, LANES), F32)
    parcels = ("v", (sh.ndev, sh.t_rows, LANES), F32)
    columns = ("v", (sh.sum_rows, LANES), F32)
    q_shape = ("v", (sh.piece, LANES), F32)
    field_shape = ("v", (modes + 1,) + rows, F32)
    t_scratch = pltpu.VMEM((sh.t_rows, LANES), F32)
    ops = dual_ops.reshape(subs * sh.rows, sh.order)
    ops_kept = ("k", ops.shape, BF16)
    ops_sems = subs // sh.group
    long = dual_ops.size * 2

    def exchange(parcel):
        return lax.all_to_all(parcel, AXES, 0, 0)

    def stack(count):
        return (count,) + rows

    parcel_shape = ("v", (sh.parcel + sh.factor_rows, LANES), F32)
    load = rigid_load[None, :]
    (t_part,) = call(
        start_kernel, "shh", [columns],
        [pltpu.VMEM(load.shape, F32), pltpu.VMEM(coarse_factor.shape, F32)]
        + [pltpu.SemaphoreType.DMA((2,))],
        mode_count, load, coarse_factor, name="start", cost=100_000,
    )
    t_sum = t_part + permute(t_part, lambda i, j: (i ^ 1, j))
    raw = (rigid_traces, dual_rhs, send_list, coarse_factor)
    fields, parcel_a, parcel_b, factor = call(
        pack_kernel, "shhhhv",
        [field_shape, parcel_shape, parcel_shape, ("v", (sh.factor_rows, LANES), F32)],
        [pltpu.VMEM((sh.slot_lanes, LANES), F32)]
        + [pltpu.VMEM(x.shape, x.dtype) for x in raw]
        + [pltpu.SemaphoreType.DMA((len(raw),))],
        mode_count, *raw, t_part, name="pack", cost=8_000_000,
    )
    parcel_a, parcel_b, factor, t_sum = lax.optimization_barrier(
        (parcel_a, parcel_b, factor, t_sum)
    )
    near_a, near_b = swap_a(parcel_a), swap_b(parcel_b)
    factor_x = x_swaps(factor)
    sum_steps = [2**k for k in range(1, (lax.axis_size("sub") - 1).bit_length())]
    for step in sum_steps[:-1]:
        t_sum = t_sum + permute(t_sum, lambda i, j: (i ^ step, j))
    ops_vmem, t_same = call(
        load_kernel, "hv", [ops_kept, columns], [pltpu.SemaphoreType.DMA((ops_sems,))],
        ops, t_sum, name="load", cost=long,
    )
    for step in sum_steps[-1:]:
        t_same = t_same + permute(t_sum, lambda i, j: (i ^ step, j))
    t_sum = t_same

    halves = core_swap(jnp.concatenate([near_a[: sh.names_at], near_b[: sh.names_at]], axis=0))
    factor_ab = jnp.concatenate([near_a[sh.parcel :], near_b[sh.parcel :], t_sum], axis=0)
    pair_rows = 2 * sh.factor_rows
    w0, sums = [factor, factor_ab[:pair_rows]], [t_sum]
    for own, pair in zip(factor_x, x_swaps(factor_ab)):
        w0 += [own, pair[:pair_rows]]
        sums.append(pair[pair_rows:])
    traces, far_traces, jumper, far_pick, far_put = call(
        setup_kernel, "vvvvv",
        [
            field_shape, field_shape,
            ("v", (sh.all_rows, 3 * sh.crs * sh.piece), BF16),
            ("v", (sh.all_rows, 3 * sh.pad), BF16),
            ("v", (3 * sh.pad, sh.piece), BF16),
        ],
        [pltpu.VMEM(rows, F32)],
        partner, fields, near_a, near_b, halves, name="setup", cost=6_000_000,
    )
    w0 = jnp.concatenate(w0 + sums + [far_traces[0, :8]], axis=0)
    w1 = core_swap(w0)
    lam0, q, t_part = call(
        first_kernel, "vvvvvvv",
        [("v", rows, F32), q_shape, parcels],
        [t_scratch],
        traces, far_traces, far_pick, far_put, w0, w1, ops_vmem, name="first", cost=long,
    )
    q0, q1 = spread_pieces(q)
    t_in = exchange(t_part)

    state0, tr0, q, ops_vmem = call(
        second_kernel, "vvvvvvvvvvh",
        [("v", stack(4), F32), t_shape, ("v", (sh.piece + sh.row_sums, LANES), F32), ops_kept],
        [t_scratch, t_scratch, pltpu.SemaphoreType.DMA((ops_sems,))],
        traces, far_traces, jumper, far_pick, far_put, q0, q1, t_in, w0, w1, ops,
        name="second", cost=long,
    )
    q0, q1 = spread_pieces(q)
    sub_parcels = ("v", (lax.axis_size("sub"), sh.t_rows, LANES), F32)
    applied, t_part = call(
        square_kernel, "vvv", [("v", rows, F32), sub_parcels], [],
        jumper, q0, q1, name="square", cost=2_000_000,
    )
    t_in = lax.all_to_all(t_part, "sub", 0, 0)

    state1, tr1, q, t_part = call(
        third_kernel, "vvvvvvvvvvvv",
        [("v", stack(3), F32), t_shape, q_shape, parcels],
        [t_scratch, pltpu.VMEM(rows, F32)],
        traces, far_traces, far_pick, far_put, applied, t_in, w0, w1, tr0, state0, lam0, ops_vmem,
        name="third", cost=long,
    )
    q0, q1 = spread_pieces(q)
    t_in = exchange(t_part)

    return tuple(
        call(
            last_kernel, "vvvvvvvvvvv",
            [("v", (subs, sh.order), F32)] * 2,
            [t_scratch],
            traces, far_traces, jumper, far_pick, q0, q1, t_in, w0, w1, tr1, state1,
            name="last", cost=4_000_000,
        )
    )


def body(*args):
    dual_ops, _, _, partner = args[:4]
    crs_num, sub_num = lax.axis_size("crs"), lax.axis_size("sub")
    whole_blocks = (
        dual_ops.shape[2] // partner.shape[1] == LANES and dual_ops.shape[1] % LANES == 0
    )
    fits = whole_blocks and args[2].shape[1] % LANES + 8 <= LANES
    fits = fits and sub_num & (sub_num - 1) == 0
    fits = fits and args[1].shape[1] <= LANES
    if fits and crs_num % 2 == 0 and crs_num & (crs_num - 1) == 0 and sub_num % 2 == 0:
        return local(*args)
    return plain(*args)


def solution(mesh):
    return jax.shard_map(
        body,
        mesh=mesh,
        in_specs=(
            P("sub", "crs", None),
            P("sub", None, None),
            P("sub", "crs"),
            P("sub", None),
            P("sub", None),
            P("sub"),
            P("sub", None),
            P("sub"),
        ),
        out_specs=(P("sub", None), P("sub", None)),
        check_vma=False,
    )
```
